128 devices in a mesh: dp: 8 (over y, core), enc: 16 (over x, z).
Axes of the slice: x: 4, y: 4, z: 4, core: 2. Of those that a mesh axis runs over, the one named last changes fastest.
Arguments:
- hidden: bfloat16 [2048, 8192], P('dp', 'enc'), may hold values from -8 to 8
- encodings: bfloat16 [16, 128, 8192], P('dp', None, 'enc'), may hold values from -8 to 8
- query_weight: bfloat16 [8192, 4096], P('enc')
- key_weight: bfloat16 [8192, 4096], P('enc')
- value_weight: bfloat16 [8192, 4096], P('enc'), may hold values from -0.0625 to 0.0625
- out_weight: bfloat16 [4096, 8192], P(None, 'enc'), may hold values from -0.09375 to 0.09375
- out_cotangent: bfloat16 [2048, 8192], P('dp', 'enc'), may hold values from -6 to 6
- stretch_nbrs: int32 [32, 2], P('dp'), may hold values from 0 to 15, all different within a row
- nbr_blocks: int32 [16], replicated, may hold values from 1 to 8, as said below
Outputs:
- layer_out: float32 [2048, 8192], P('dp', 'enc')
- grad_hidden: float32 [2048, 8192], P('dp', 'enc')
- grad_encodings: float32 [16, 128, 8192], P('dp', None, 'enc')
- grad_query_weight: float32 [8192, 4096], P('enc', 'dp')
- grad_key_weight: float32 [8192, 4096], P('enc', 'dp')
- grad_value_weight: float32 [8192, 4096], P('enc', 'dp')
- grad_out_weight: float32 [4096, 8192], P('dp', 'enc')
The draws below stay inside these ranges and needn't reach their ends.
Inputs may be any that keep to these rules, and one draw needn't show every extreme that they name: `stretch_nbrs`: each stretch names two different neighbours, and every neighbour is named by some stretch. Neighbour n holds 16 * nbr_blocks[n] valid token slots at its start; some neighbour is full.
All inputs are finite; a program needn't handle non-finite values.
Results may differ from the reference program's by a relative error of at most 0.022.
The reference program's roundings to bfloat16 on the way (of `queries`, `key_rows`, `heads_out`, `grad_heads`, `grad_scores`, `grad_query` and `grad_keys`) count: a program that leaves them out, or rounds other values in their place, can miss the bound.
Values may be sent and summed in bfloat16 or wider, within the bound.
A program may use at most 128 MiB of HBM per device.

```python
import jax
import jax.numpy as jnp
from jax import lax

D = 8192
HEADS = 32
HD = 128
STRETCH = 64
R = 128
BLK = 16
CH_DP = 4
STRETCHES = 32
TOKENS = 2048
NEIGH = 16
N_DP = 8
N_ENC = 16


def shared_query(key):
    return jnp.clip(jax.random.normal(jax.random.fold_in(key, 202), (D, HEADS * HD), jnp.float32), -6.0, 6.0) * D ** (-0.5)


def draw_hidden(key, part):
    key = jax.random.fold_in(key, 1)
    values = jnp.clip(jax.random.normal(key, (TOKENS, D), jnp.float32), -6.0, 6.0)
    return values.astype(jnp.bfloat16)


def draw_encodings(key, part):
    key = jax.random.fold_in(key, 2)
    values = jnp.clip(jax.random.normal(key, (NEIGH, R, D), jnp.float32), -6.0, 6.0)
    return values.astype(jnp.bfloat16)


def draw_query_weight(key, part):
    base = shared_query(key)
    return base.astype(jnp.bfloat16)


def draw_key_weight(key, part):
    key = jax.random.fold_in(key, 4)
    noise = jnp.clip(jax.random.normal(key, (D, HEADS * HD), jnp.float32), -6.0, 6.0) * D ** (-0.5)
    return noise.astype(jnp.bfloat16)


def draw_nbr_blocks(key, part):
    key = jax.random.fold_in(key, 3)
    first_key, second_key = jax.random.split(key)
    counts = jax.random.randint(first_key, (NEIGH,), 1, R // BLK + 1)
    full_one = jax.random.randint(second_key, (), 0, NEIGH)
    return jnp.where(jnp.arange(NEIGH) == full_one, R // BLK, counts).astype(jnp.int32)


def shard_levels(key, extent, pieces, least, top_value):
    loudness = 1.0
    for position, shards_of in pieces:
        draws = jax.random.uniform(jax.random.fold_in(jax.random.fold_in(key, 6), position), (shards_of,), jnp.float32, least / len(pieces), top_value / len(pieces))
        loudness = loudness * jnp.repeat(jnp.exp(draws), extent[position] // shards_of).reshape((-1,) + (1,) * (len(extent) - 1 - position))
    return loudness


def choose_distinct(stream_key, rows, count, top, lift):
    sequence = jax.random.permutation(jax.random.fold_in(stream_key, 1), count)
    favour = sequence
    for power in range(3):
        favour = favour * favour // count
    favour = favour * lift // count
    chance = jax.random.randint(jax.random.fold_in(stream_key, 2), (rows, count), 0, 4096) + favour
    sure = jax.random.permutation(jax.random.fold_in(stream_key, 3), rows)[jnp.arange(count) % rows]
    chance = jnp.where(jnp.arange(rows)[:, None] == sure[None, :], 1 << 14, chance)
    priority = chance * count + jnp.arange(count)
    return lax.top_k(priority.astype(jnp.int32), top)[1].astype(jnp.int32)


def scatter_about(rng, dims, deviation, limit, cuts=(), kind=jnp.bfloat16):
    drawn = deviation * jax.random.normal(rng, dims, jnp.float32)
    if cuts:
        drawn = drawn * shard_levels(rng, dims, cuts, -0.22, 0.18)
    return jnp.clip(drawn, -limit, limit).astype(kind)


def setup_inputs(seed: int = 0) -> dict:
    arg_keys = jax.random.split(jax.random.key(seed), 10)
    hidden = draw_hidden(jax.random.fold_in(arg_keys[9], 71), 0)
    encodings = draw_encodings(jax.random.fold_in(arg_keys[9], 71), 0)
    query_weight = draw_query_weight(jax.random.fold_in(arg_keys[9], 71), 0)
    key_weight = draw_key_weight(jax.random.fold_in(arg_keys[9], 71), 0)
    value_weight = scatter_about(arg_keys[4], (D, HEADS * HD), D ** -0.5, 0.0625, ((0, 16),))
    out_weight = scatter_about(arg_keys[5], (HEADS * HD, D), (HEADS * HD) ** -0.5, 0.09375, ((1, 16),))
    out_cotangent = scatter_about(arg_keys[6], (TOKENS, D), 1.0, 6.0, ((0, 8), (1, 16)))
    stretch_nbrs = choose_distinct(arg_keys[7], STRETCHES, NEIGH, 2, 2048)
    nbr_blocks = draw_nbr_blocks(jax.random.fold_in(arg_keys[9], 71), 0)
    return dict(hidden=hidden, encodings=encodings, query_weight=query_weight, key_weight=key_weight, value_weight=value_weight, out_weight=out_weight, out_cotangent=out_cotangent, stretch_nbrs=stretch_nbrs, nbr_blocks=nbr_blocks)


HIGH = lax.Precision.HIGHEST


def rounded(product_term):
    return lax.optimization_barrier(product_term.astype(jnp.bfloat16)).astype(jnp.float32)


def block_sum(left_rows, right_rows):
    slice_width = left_rows.shape[1] // N_ENC
    left_blocks = left_rows.reshape(left_rows.shape[0], N_ENC, slice_width)
    right_blocks = right_rows.reshape(N_ENC, slice_width, right_rows.shape[1])

    def accumulate(running, slot_index):
        portion = lax.dynamic_index_in_dim(left_blocks, slot_index, 1, keepdims=False)
        weight = lax.dynamic_index_in_dim(right_blocks, slot_index, 0, keepdims=False)
        return running + rounded(jnp.dot(portion, weight, preferred_element_type=jnp.float32)), None

    zeros_init = jnp.zeros((left_rows.shape[0], right_rows.shape[1]), jnp.float32)
    running, _ = lax.scan(accumulate, zeros_init, jnp.arange(N_ENC, dtype=jnp.int32))
    return running.astype(jnp.bfloat16)


def group_sum(left_rows, right_rows):
    left_blocks = left_rows.reshape(N_DP, -1, left_rows.shape[1])
    right_blocks = right_rows.reshape(N_DP, -1, right_rows.shape[1])

    def accumulate(running, pair_terms):
        product_term = lax.dot_general(pair_terms[0], pair_terms[1], (((0,), (0,)), ((), ())), preferred_element_type=jnp.float32)
        return running + rounded(product_term), None

    zeros_init = jnp.zeros((left_rows.shape[1], right_rows.shape[1]), jnp.float32)
    running, _ = lax.scan(accumulate, zeros_init, (left_blocks, right_blocks))
    return running


def attend(queries, key_rows, value_rows, key_valid, score_scale):
    scores = jnp.einsum("cthk,cjrhk->chjtr", queries.astype(jnp.float32), key_rows.astype(jnp.float32)) * score_scale
    key_mask = key_valid[:, None, :, None, :]
    row_max = jnp.max(jnp.where(key_mask, scores, -1.0e30), axis=4)
    exp_terms = jnp.where(key_mask, jnp.exp(scores - row_max[..., None]), 0.0)
    row_total = jnp.sum(exp_terms, axis=4)
    partial_value = jnp.einsum("chjtr,cjrhk->chjtk", rounded(exp_terms), value_rows.astype(jnp.float32))
    best_max = jnp.max(row_max, axis=2, keepdims=True)
    factor = jnp.exp(row_max - best_max)
    denominator = jnp.sum(factor * row_total, axis=2)
    output = jnp.sum(factor[..., None] * partial_value, axis=2) / denominator[..., None]
    return output, exp_terms, factor, denominator


def attend_back(queries, key_rows, value_rows, score_scale, exp_terms, factor, denominator, grad_blocks):
    weights = factor[..., None] * exp_terms / denominator[:, :, None, :, None]
    grad_f32 = grad_blocks.astype(jnp.float32)
    value_contrib = jnp.einsum("chjtr,cthk->cjrhk", rounded(weights), grad_f32)
    grad_probs = jnp.einsum("cthk,cjrhk->chjtr", grad_f32, value_rows.astype(jnp.float32))
    row_inner = jnp.sum(weights * grad_probs, axis=(2, 4), keepdims=True)
    grad_scores = rounded(weights * (grad_probs - row_inner) * score_scale)
    grad_q = jnp.einsum("chjtr,cjrhk->cthk", grad_scores, key_rows.astype(jnp.float32))
    key_contrib = jnp.einsum("chjtr,cthk->cjrhk", grad_scores, queries.astype(jnp.float32))
    return grad_q, key_contrib, value_contrib


def reference(hidden, encodings, query_weight, key_weight, value_weight, out_weight, out_cotangent, stretch_nbrs, nbr_blocks):
    score_scale = HD ** -0.5
    flat_enc = encodings.reshape(NEIGH * R, D)
    queries = block_sum(hidden, query_weight)
    key_rows = block_sum(flat_enc, key_weight)
    value_rows = block_sum(flat_enc, value_weight)
    onehot = stretch_nbrs[:, :, None] == jnp.arange(NEIGH, dtype=jnp.int32)[None, None, :]
    limits = BLK * jnp.sum(jnp.where(onehot, nbr_blocks[None, None, :], 0), axis=2)
    key_valid = jnp.arange(R, dtype=jnp.int32)[None, None, :] < limits[:, :, None]
    query_blocks = queries.reshape(STRETCHES, STRETCH, HEADS, HD)
    key_picked = key_rows.reshape(NEIGH, R, HEADS, HD)[stretch_nbrs]
    value_picked = value_rows.reshape(NEIGH, R, HEADS, HD)[stretch_nbrs]
    output, exp_terms, factor, denominator = attend(query_blocks, key_picked, value_picked, key_valid, score_scale)
    heads_out = output.transpose(0, 2, 1, 3).reshape(TOKENS, HEADS * HD).astype(jnp.bfloat16)
    layer_out = jnp.dot(heads_out, out_weight, preferred_element_type=jnp.float32)
    grad_heads = lax.dot_general(out_cotangent, out_weight, (((1,), (1,)), ((), ())), preferred_element_type=jnp.float32).astype(jnp.bfloat16)
    grad_blocks = grad_heads.reshape(STRETCHES, STRETCH, HEADS, HD)
    grad_q, key_contrib, value_contrib = attend_back(query_blocks, key_picked, value_picked, score_scale, exp_terms, factor, denominator, grad_blocks)
    grad_query = grad_q.reshape(TOKENS, HEADS * HD).astype(jnp.bfloat16)
    select = onehot.astype(jnp.float32).reshape(N_DP, CH_DP, 2, NEIGH)

    def neighbour_sum(contrib):
        grouped = contrib.reshape(N_DP, CH_DP, 2, R, HEADS * HD)
        dense_grads = jnp.einsum("gcjn,gcjrk->gnrk", select, grouped, precision=HIGH)
        return jnp.sum(rounded(dense_grads), axis=0).astype(jnp.bfloat16).reshape(NEIGH * R, HEADS * HD)

    grad_keys = neighbour_sum(key_contrib)
    grad_values = neighbour_sum(value_contrib)
    grad_hidden = lax.dot_general(grad_query, query_weight, (((1,), (1,)), ((), ())), preferred_element_type=jnp.float32)
    enc_sum = lax.dot_general(grad_keys, key_weight, (((1,), (1,)), ((), ())), preferred_element_type=jnp.float32)
    enc_sum = enc_sum + lax.dot_general(grad_values, value_weight, (((1,), (1,)), ((), ())), preferred_element_type=jnp.float32)
    grad_encodings = enc_sum.reshape(NEIGH, R, D)
    grad_query_weight = group_sum(hidden, grad_query)
    grad_key_weight = group_sum(flat_enc, grad_keys)
    grad_value_weight = group_sum(flat_enc, grad_values)
    grad_out_weight = group_sum(heads_out, out_cotangent)
    return layer_out, grad_hidden, grad_encodings, grad_query_weight, grad_key_weight, grad_value_weight, grad_out_weight
```

```python
import functools

import jax
import jax.numpy as jnp
from jax import lax
from jax.experimental import pallas as pl
from jax.experimental.pallas import tpu as pltpu
from jax.sharding import PartitionSpec as P

HD = 128
BLK = 16
MESH = pl.DeviceIdType.MESH
F32 = jnp.float32
BF16 = jnp.bfloat16
NT = (((1,), (1,)), ((), ()))
TN = (((0,), (0,)), ((), ()))


def mm(a, b):
    return jnp.dot(a, b, preferred_element_type=F32)


class Place:
    def __init__(self):
        self.dp = lax.axis_index("dp")
        self.enc = lax.axis_index("enc")
        dp, enc = self.dp, self.enc
        self.y, self.c = dp // 2, dp % 2
        self.x, self.z = enc // 4, enc % 4
        x, y, z, c = self.x, self.y, self.z, self.c
        self.right = {
            "x": (dp, ((x + 1) % 4) * 4 + z),
            "z": (dp, x * 4 + (z + 1) % 4),
            "y": (((y + 1) % 4) * 2 + c, enc),
        }
        self.left = {
            "x": (dp, ((x + 3) % 4) * 4 + z),
            "z": (dp, x * 4 + (z + 3) % 4),
            "y": (((y + 3) % 4) * 2 + c, enc),
        }
        self.pos = {"x": x, "y": y, "z": z}
        self.partner = (y * 2 + (1 - c), enc)

    def barrier(self):
        sem = pltpu.get_barrier_semaphore()
        others = list(self.right.values()) + list(self.left.values()) + [self.partner]
        for other in others:
            pl.semaphore_signal(sem, inc=1, device_id=other, device_id_type=MESH)
        pl.semaphore_wait(sem, len(others))


class Copies:
    def __init__(self, send_sems, recv_sems):
        self.send_sems, self.recv_sems, self.used, self.started = send_sems, recv_sems, 0, []

    def start(self, src, dst, device):
        k = self.used
        self.used += 1
        copy = pltpu.make_async_remote_copy(
            src_ref=src,
            dst_ref=dst,
            send_sem=self.send_sems.at[k],
            recv_sem=self.recv_sems.at[k],
            device_id=device,
            device_id_type=MESH,
        )
        copy.start()
        self.started.append(copy)
        return copy

    def finish(self):
        for copy in self.started:
            copy.wait_send()


class RingSum:
    def __init__(self, copies, place, axis, part, r1, r2):
        self.copies, self.part, self.r1, self.r2 = copies, part, r1, r2
        self.right, self.left = place.right[axis], place.left[axis]
        pos = place.pos[axis]
        self.pos, self.rt, self.lf, self.opp = pos, (pos + 1) % 4, (pos + 3) % 4, (pos + 2) % 4

    def send_opposite(self):
        self.a = self.copies.start(self.part(self.opp, 0), self.r1.at[0], self.right)
        self.b = self.copies.start(self.part(self.opp, 1), self.r1.at[1], self.left)

    def send_right(self):
        self.d = self.copies.start(self.part(self.rt, 1), self.r2.at[0, 1], self.right)

    def send_left(self):
        self.e = self.copies.start(self.part(self.lf, 0), self.r2.at[1, 0], self.left)

    def first(self):
        self.send_opposite()
        self.send_right()
        self.send_left()

    def second(self):
        self.a.wait_recv()
        mine = self.part(self.rt, 0)
        mine[...] = (mine[...].astype(F32) + self.r1[0].astype(F32)).astype(BF16)
        self.f = self.copies.start(mine, self.r2.at[0, 0], self.right)
        self.b.wait_recv()
        mine = self.part(self.lf, 1)
        mine[...] = (mine[...].astype(F32) + self.r1[1].astype(F32)).astype(BF16)
        self.g = self.copies.start(mine, self.r2.at[1, 1], self.left)

    def total(self):
        for copy in (self.d, self.e, self.f, self.g):
            copy.wait_recv()
        return [
            self.part(self.pos, h)[...].astype(F32)
            + self.r2[0, h].astype(F32)
            + self.r2[1, h].astype(F32)
            for h in (0, 1)
        ]


class RingGather:
    def __init__(self, copies, place, axis, block):
        self.copies, self.block = copies, block
        self.right, self.left = place.right[axis], place.left[axis]
        pos = place.pos[axis]
        self.pos, self.rt, self.lf = pos, (pos + 1) % 4, (pos + 3) % 4

    def first(self):
        own = self.block(self.pos, None)
        self.a = self.copies.start(own, own, self.right)
        self.b = self.copies.start(own, own, self.left)

    def second(self):
        self.a.wait_recv()
        part = self.block(self.lf, 0)
        self.d = self.copies.start(part, part, self.right)
        self.b.wait_recv()
        part = self.block(self.rt, 1)
        self.e = self.copies.start(part, part, self.left)

    def done(self):
        self.d.wait_recv()
        self.e.wait_recv()


HALVES = ((0, 128), (128, 256))


class PlaneSum:
    def __init__(self, copies, place, terms, sums, r1a, r2a, r1b, r2b):
        x, z = place.pos["x"], place.pos["z"]
        self.sums, self.place = sums, place

        def upper(b, h):
            return terms.at[b, 2 * h : 2 * h + 2, 0:128]

        def lower(b, h):
            return terms.at[2 * h : 2 * h + 2, b, 128:256]

        self.one = (
            RingSum(copies, place, "x", upper, r1a.at[0], r2a.at[0]),
            RingSum(copies, place, "z", lower, r1a.at[1], r2a.at[1]),
        )

        def upper_two(b, h):
            return sums.at[0, b, 64 * h : 64 * h + 64]

        def lower_two(b, h):
            return sums.at[1, b, 64 * h : 64 * h + 64]

        self.two = (
            RingSum(copies, place, "z", upper_two, r1b.at[0], r2b.at[0]),
            RingSum(copies, place, "x", lower_two, r1b.at[1], r2b.at[1]),
        )

    def step1(self):
        for ring in self.one:
            ring.first()

    def step2(self):
        for ring in self.one:
            ring.second()

    def step3(self):
        for k in (0, 1):
            low, high = self.one[k].total()
            self.sums[k, 0:2] = low.astype(BF16)
            self.sums[k, 2:4] = high.astype(BF16)
            self.two[k].first()

    def step4(self):
        for ring in self.two:
            ring.second()

    def finish(self, store):
        for k in (0, 1):
            low, high = self.two[k].total()
            store(k * 128, low.astype(BF16))
            store(k * 128 + 64, high.astype(BF16))


class PlaneGather:
    def __init__(self, copies, place, buf):
        x, z = place.pos["x"], place.pos["z"]

        def upper(b, h):
            if h is None:
                return buf.at[b, z, 0:128]
            return buf.at[b, z, 64 * h : 64 * h + 64]

        def lower(b, h):
            if h is None:
                return buf.at[x, b, 128:256]
            return buf.at[x, b, 128 + 64 * h : 192 + 64 * h]

        def upper_two(b, h):
            if h is None:
                return buf.at[:, b, 0:128]
            return buf.at[2 * h : 2 * h + 2, b, 0:128]

        def lower_two(b, h):
            if h is None:
                return buf.at[b, :, 128:256]
            return buf.at[b, 2 * h : 2 * h + 2, 128:256]

        self.one = (
            RingGather(copies, place, "x", upper),
            RingGather(copies, place, "z", lower),
        )
        self.two = (
            RingGather(copies, place, "z", upper_two),
            RingGather(copies, place, "x", lower_two),
        )

    def step1(self):
        for ring in self.one:
            ring.first()

    def step2(self):
        for ring in self.one:
            ring.second()

    def step3(self):
        for one, two in zip(self.one, self.two):
            one.done()
            two.first()

    def step4(self):
        for ring in self.two:
            ring.second()

    def done(self):
        for ring in self.two:
            ring.done()


def project_kernel(
    hidden,
    encodings,
    cotangent,
    wk_hbm,
    wv_hbm,
    wq_hbm,
    wo_hbm,
    queries_out,
    grad_out,
    pair_out,
    weights,
    out_weight,
    terms,
    sums,
    r1a,
    r2a,
    r1b,
    r2b,
    pair,
    load_sems,
    send_sems,
    recv_sems,
):
    place = Place()
    copies = Copies(send_sems, recv_sems)
    loads = [
        pltpu.make_async_copy(src, weights.at[k], load_sems.at[k])
        for k, src in enumerate((wk_hbm, wv_hbm, wq_hbm))
    ]
    for load in loads:
        load.start()
    load_out = pltpu.make_async_copy(wo_hbm, out_weight, load_sems.at[3])
    place.barrier()
    left = (encodings, encodings, hidden)
    rings = [
        PlaneSum(
            copies, place, terms.at[k], sums.at[k], r1a.at[k], r2a.at[k], r1b.at[k], r2b.at[k]
        )
        for k in range(4)
    ]

    def make_terms(k):
        loads[k].wait()
        rows = left[k][...]

        def body(x, carry):
            columns = pl.ds(pl.multiple_of(x * 1024, 1024), 1024)
            product = mm(rows, weights[k, :, columns]).astype(BF16)
            for z in range(4):
                terms[k, x, z] = product[:, z * 256 : z * 256 + 256]
            return carry

        lax.fori_loop(0, 4, body, 0)

    def make_grad_terms():
        load_out.wait()
        rows = cotangent[...]

        def body(x, carry):
            for z in range(4):
                span = pl.ds(pl.multiple_of(x * 1024 + z * 256, 256), 256)
                product = lax.dot_general(rows, out_weight[span, :], NT, preferred_element_type=F32)
                terms[3, x, z] = product.astype(BF16)
            return carry

        lax.fori_loop(0, 4, body, 0)

    def pair_block(k):
        def block(b, h):
            if h is None:
                return pair.at[k, b, place.c]
            return pair.at[k, b, place.c, 128 * h : 128 * h + 128]

        return block

    gathers = [RingGather(copies, place, "y", pair_block(k)) for k in (0, 1)]

    def store_pair(k):
        def store(row, value):
            pair[k, place.y, place.c, row : row + 64] = value

        return store

    def store_queries(row, value):
        queries_out[row : row + 64] = value

    def store_grad(row, value):
        grad_out[row : row + 64] = value

    def swap(k):
        gathers[k].done()
        mine = pair.at[k, :, place.c]
        return copies.start(mine, mine, place.partner)

    keys, values, query, grad = rings
    make_terms(0)
    load_out.start()
    keys.step1()
    make_terms(1)
    values.step1()
    make_terms(2)
    keys.step2()
    query.step1()
    values.step2()
    make_grad_terms()
    keys.step3()
    values.step3()
    grad.step1()
    keys.step4()
    query.step2()
    values.step4()
    keys.finish(store_pair(0))
    gathers[0].first()
    values.finish(store_pair(1))
    gathers[1].first()
    query.step3()
    grad.step2()
    gathers[0].second()
    query.step4()
    gathers[1].second()
    grad.step3()
    swap_keys = swap(0)
    query.finish(store_queries)
    swap_values = swap(1)
    grad.step4()
    swap_keys.wait_recv()
    pair_out[0] = pair[0]
    swap_values.wait_recv()
    pair_out[1] = pair[1]
    grad.finish(store_grad)
    copies.finish()


def attend_kernel(
    nbrs, blocks, queries, grads, pair, heads_out, query_grads, dense_out, prob, dense
):
    scale = HD ** (-0.5)
    dense[...] = jnp.zeros_like(dense)
    cases = [(c, h) for c in range(4) for h in range(2)]

    def rows(ref, c, h):
        return ref[c * 64 : c * 64 + 64, h * 128 : h * 128 + 128]

    def picked(which, c, h):
        return jnp.concatenate(
            [pair[which, nbrs[c, j], :, h * 128 : h * 128 + 128] for j in (0, 1)], axis=0
        )

    slot = lax.broadcasted_iota(jnp.int32, (64, 256), 1)
    for i, (c, h) in enumerate(cases):
        limit0 = BLK * blocks[nbrs[c, 0]]
        limit1 = BLK * blocks[nbrs[c, 1]]
        valid = slot < jnp.where(slot < 128, limit0, limit1 + 128)
        scores = (
            lax.dot_general(rows(queries, c, h), picked(0, c, h), NT, preferred_element_type=F32)
            * scale
        )
        scores = jnp.where(valid, scores, -1e30)
        top = jnp.max(scores, axis=1, keepdims=True)
        terms = jnp.where(valid, jnp.exp(scores - top), 0.0)
        total = jnp.sum(terms, axis=1, keepdims=True)
        values = picked(1, c, h)
        output = mm(terms.astype(BF16), values) / total
        heads_out[c * 64 : c * 64 + 64, h * 128 : h * 128 + 128] = output.astype(BF16)
        prob[i] = terms / total
    for i, (c, h) in enumerate(cases):
        weights = prob[i]
        grad = rows(grads, c, h)
        keys = picked(0, c, h)
        value_part = lax.dot_general(weights.astype(BF16), grad, TN, preferred_element_type=F32)
        grad_prob = lax.dot_general(grad, picked(1, c, h), NT, preferred_element_type=F32)
        inner = jnp.sum(weights * grad_prob, axis=1, keepdims=True)
        grad_scores = (weights * (grad_prob - inner) * scale).astype(BF16)
        query_grads[c * 64 : c * 64 + 64, h * 128 : h * 128 + 128] = mm(grad_scores, keys).astype(
            BF16
        )
        key_part = lax.dot_general(
            grad_scores, rows(queries, c, h), TN, preferred_element_type=F32
        )
        for j in (0, 1):
            n = nbrs[c, j]
            dense[0, n, :, h * 128 : h * 128 + 128] += key_part[j * 128 : j * 128 + 128]
            dense[1, n, :, h * 128 : h * 128 + 128] += value_part[j * 128 : j * 128 + 128]
    dense_out[...] = dense[...].astype(BF16)


def finish_kernel(
    heads,
    query_grads,
    dense,
    hidden,
    encodings,
    cotangent,
    wo_hbm,
    wq_hbm,
    wk_hbm,
    wv_hbm,
    layer_out,
    grad_hidden,
    grad_encodings,
    grad_wq,
    grad_wk,
    grad_wv,
    grad_wo,
    weights,
    out_weight,
    gathered,
    theirs,
    sides,
    side_t,
    dense_in,
    dense_sum,
    dense_r1,
    dense_r2,
    parts,
    part_r1,
    part_r2,
    load_sems,
    send_sems,
    recv_sems,
):
    place = Place()
    x, y, z, c = place.x, place.y, place.z, place.c
    copies = Copies(send_sems, recv_sems)
    load_wo = pltpu.make_async_copy(wo_hbm, out_weight, load_sems.at[0])
    load_wq = pltpu.make_async_copy(wq_hbm, weights.at[1], load_sems.at[1])
    load_wk = pltpu.make_async_copy(wk_hbm, weights.at[0], load_sems.at[2])
    load_wv = pltpu.make_async_copy(wv_hbm, weights.at[1], load_sems.at[3])
    load_wo.start()
    load_wq.start()
    load_wk.start()
    gathered[0, x, z] = heads[...]
    gathered[1, x, z] = query_grads[...]
    place.barrier()
    nets = [PlaneGather(copies, place, gathered.at[k]) for k in range(4)]
    net_h, net_q, net_k, net_v = nets
    swap_dense = copies.start(dense.at[:, :, 1 - c], dense_in, place.partner)
    net_h.step1()
    net_q.step1()
    for k, ref in enumerate((cotangent, hidden, encodings)):
        sides[k, 0] = ref[...]
    swap_sides = copies.start(sides.at[:, 0], sides.at[:, 1], place.partner)

    def dense_part(b, h):
        return dense_sum.at[b, h]

    ring_dense = RingSum(copies, place, "y", dense_part, dense_r1, dense_r2)
    swap_dense.wait_recv()
    for h in (0, 1):
        for b in range(4):
            dense_sum[b, h] = (
                dense[h, b, c].astype(F32) + dense_in[h, b].astype(F32)
            ).astype(BF16)
    ring_dense.first()
    net_h.step2()
    net_q.step2()
    ring_dense.second()
    net_h.step3()
    net_q.step3()
    swap_sides.wait_recv()
    for k in range(3):
        for side in (0, 1):
            side_t[k, :, side * 256 : side * 256 + 256] = sides[k, side].T
    key_sum, value_sum = ring_dense.total()
    gathered[2, x, z] = key_sum.astype(BF16)
    gathered[3, x, z] = value_sum.astype(BF16)
    net_k.step1()
    net_v.step1()
    net_h.step4()
    net_q.step4()

    def swap_half(k):
        return copies.start(
            gathered.at[k, :, pl.ds(2 * (1 - c), 2)], theirs.at[k], place.partner
        )

    def ring_of(k):
        def part(b, h):
            return parts.at[k, b, 256 * h : 256 * h + 256]

        return RingSum(copies, place, "y", part, part_r1.at[k], part_r2.at[k])

    def weight_grad(k, side, ring):
        def block(b):
            own = jnp.concatenate([gathered[k, b, 2 * c + i] for i in (0, 1)], axis=1)
            other = jnp.concatenate([theirs[k, b, i] for i in (0, 1)], axis=1)
            both = jnp.concatenate([own, other], axis=0)
            parts[k, b] = mm(side_t[side], both).astype(BF16)

        block(ring.opp)
        ring.send_opposite()
        block(ring.rt)
        ring.send_right()
        block(ring.lf)
        ring.send_left()
        block(ring.pos)

    def wide(k, b):
        return jnp.concatenate([gathered[k, b, i] for i in range(4)], axis=1)

    def columns(b):
        return pl.ds(pl.multiple_of(b * 1024, 1024), 1024)

    def accumulate(out, make):
        out[...] = make(0)

        def body(b, carry):
            out[...] += make(b)
            return carry

        lax.fori_loop(1, 4, body, 0)

    def transposed(k, slot, b):
        return lax.dot_general(
            wide(k, b), weights[slot, :, columns(b)], NT, preferred_element_type=F32
        )

    net_h.done()
    swap_h = swap_half(0)
    load_wo.wait()
    accumulate(layer_out, lambda b: mm(wide(0, b), out_weight[columns(b), :]))
    net_k.step2()
    net_v.step2()
    rings = [ring_of(k) for k in range(4)]
    swap_h.wait_recv()
    weight_grad(0, 0, rings[0])
    net_q.done()
    swap_q = swap_half(1)
    net_k.step3()
    net_v.step3()
    load_wq.wait()
    accumulate(grad_hidden, lambda b: transposed(1, 1, b))
    load_wv.start()
    swap_q.wait_recv()
    rings[0].second()
    weight_grad(1, 1, rings[1])
    net_k.step4()
    net_v.step4()
    low, high = rings[0].total()
    grad_wo[:, 0:256] = low.T
    grad_wo[:, 256:512] = high.T
    rings[1].second()
    net_k.done()
    swap_k = swap_half(2)
    net_v.done()
    swap_v = swap_half(3)
    swap_k.wait_recv()
    weight_grad(2, 2, rings[2])
    swap_v.wait_recv()
    low, high = rings[1].total()
    grad_wq[0:256] = low
    grad_wq[256:512] = high
    rings[2].second()
    weight_grad(3, 2, rings[3])
    load_wk.wait()
    load_wv.wait()
    accumulate(grad_encodings, lambda b: transposed(2, 0, b) + transposed(3, 1, b))
    low, high = rings[2].total()
    grad_wk[0:256] = low
    grad_wk[256:512] = high
    rings[3].second()
    low, high = rings[3].total()
    grad_wv[0:256] = low
    grad_wv[256:512] = high
    copies.finish()


def vmem():
    return pl.BlockSpec(memory_space=pltpu.VMEM)


def hbm():
    return pl.BlockSpec(memory_space=pl.ANY)


def shape(*dims, dtype=BF16):
    return jax.ShapeDtypeStruct(dims, dtype)


def per_device(
    hidden,
    encodings,
    query_weight,
    key_weight,
    value_weight,
    out_weight,
    out_cotangent,
    stretch_nbrs,
    nbr_blocks,
):
    flat_enc = encodings.reshape(256, 512)
    dma = pltpu.SemaphoreType.DMA
    limit = 60 * 1024 * 1024
    queries, grads, pair = pl.pallas_call(
        project_kernel,
        out_shape=[shape(256, 256), shape(256, 256), shape(2, 4, 2, 256, 256)],
        in_specs=[vmem()] * 3 + [hbm()] * 4,
        out_specs=[vmem()] * 3,
        scratch_shapes=[
            pltpu.VMEM((3, 512, 4096), BF16),
            pltpu.VMEM((4096, 512), BF16),
            pltpu.VMEM((4, 4, 4, 256, 256), BF16),
            pltpu.VMEM((4, 2, 4, 128, 256), BF16),
            pltpu.VMEM((4, 2, 2, 2, 128, 256), BF16),
            pltpu.VMEM((4, 2, 2, 2, 2, 128, 256), BF16),
            pltpu.VMEM((4, 2, 2, 64, 256), BF16),
            pltpu.VMEM((4, 2, 2, 2, 64, 256), BF16),
            pltpu.VMEM((2, 4, 2, 256, 256), BF16),
            dma((4,)),
            dma((112,)),
            dma((112,)),
        ],
        compiler_params=pltpu.CompilerParams(
            collective_id=0, has_side_effects=True, vmem_limit_bytes=limit
        ),
    )(hidden, flat_enc, out_cotangent, key_weight, value_weight, query_weight, out_weight)
    heads, query_grads, dense = pl.pallas_call(
        attend_kernel,
        out_shape=[shape(256, 256), shape(256, 256), shape(2, 16, 128, 256)],
        in_specs=[pl.BlockSpec(memory_space=pltpu.SMEM)] * 2 + [vmem()] * 3,
        out_specs=[vmem()] * 3,
        scratch_shapes=[
            pltpu.VMEM((8, 64, 256), F32),
            pltpu.VMEM((2, 16, 128, 256), F32),
        ],
        compiler_params=pltpu.CompilerParams(vmem_limit_bytes=limit),
    )(stretch_nbrs, nbr_blocks, queries, grads, pair.reshape(2, 16, 128, 256))
    outs = pl.pallas_call(
        finish_kernel,
        out_shape=[
            shape(256, 512, dtype=F32),
            shape(256, 512, dtype=F32),
            shape(256, 512, dtype=F32),
            shape(512, 512, dtype=F32),
            shape(512, 512, dtype=F32),
            shape(512, 512, dtype=F32),
            shape(512, 512, dtype=F32),
        ],
        in_specs=[vmem()] * 6 + [hbm()] * 4,
        out_specs=[vmem()] * 7,
        scratch_shapes=[
            pltpu.VMEM((2, 512, 4096), BF16),
            pltpu.VMEM((4096, 512), BF16),
            pltpu.VMEM((4, 4, 4, 256, 256), BF16),
            pltpu.VMEM((4, 4, 2, 256, 256), BF16),
            pltpu.VMEM((3, 2, 256, 512), BF16),
            pltpu.VMEM((3, 512, 512), BF16),
            pltpu.VMEM((2, 4, 256, 256), BF16),
            pltpu.VMEM((4, 2, 256, 256), BF16),
            pltpu.VMEM((2, 256, 256), BF16),
            pltpu.VMEM((2, 2, 256, 256), BF16),
            pltpu.VMEM((4, 4, 512, 512), BF16),
            pltpu.VMEM((4, 2, 256, 512), BF16),
            pltpu.VMEM((4, 2, 2, 256, 512), BF16),
            dma((4,)),
            dma((112,)),
            dma((112,)),
        ],
        compiler_params=pltpu.CompilerParams(
            collective_id=1, has_side_effects=True, vmem_limit_bytes=limit
        ),
    )(
        heads,
        query_grads,
        dense.reshape(2, 4, 2, 256, 256),
        hidden,
        flat_enc,
        out_cotangent,
        out_weight,
        query_weight,
        key_weight,
        value_weight,
    )
    layer_out, grad_hidden, grad_enc, grad_wq, grad_wk, grad_wv, grad_wo = outs
    return (
        layer_out,
        grad_hidden,
        grad_enc.reshape(encodings.shape),
        grad_wq,
        grad_wk,
        grad_wv,
        grad_wo,
    )


def solution(mesh):
    in_specs = (
        P("dp", "enc"),
        P("dp", None, "enc"),
        P("enc", None),
        P("enc", None),
        P("enc", None),
        P(None, "enc"),
        P("dp", "enc"),
        P("dp", None),
        P(),
    )
    out_specs = (
        P("dp", "enc"),
        P("dp", "enc"),
        P("dp", None, "enc"),
        P("enc", "dp"),
        P("enc", "dp"),
        P("enc", "dp"),
        P("dp", "enc"),
    )
    return jax.shard_map(
        per_device, mesh=mesh, in_specs=in_specs, out_specs=out_specs, check_vma=False
    )
```

```python
import functools

import jax
import jax.numpy as jnp
from jax import lax
from jax.experimental import pallas as pl
from jax.experimental.pallas import tpu as pltpu
from jax.sharding import PartitionSpec as P

HD = 128
BLK = 16
MESH = pl.DeviceIdType.MESH
F32 = jnp.float32
BF16 = jnp.bfloat16
NT = (((1,), (1,)), ((), ()))
TN = (((0,), (0,)), ((), ()))


def mm(a, b):
    return jnp.dot(a, b, preferred_element_type=F32)


class Place:
    def __init__(self):
        self.dp = lax.axis_index("dp")
        self.enc = lax.axis_index("enc")
        dp, enc = self.dp, self.enc
        self.y, self.c = dp // 2, dp % 2
        self.x, self.z = enc // 4, enc % 4
        x, y, z, c = self.x, self.y, self.z, self.c
        self.right = {
            "x": (dp, ((x + 1) % 4) * 4 + z),
            "z": (dp, x * 4 + (z + 1) % 4),
            "y": (((y + 1) % 4) * 2 + c, enc),
        }
        self.left = {
            "x": (dp, ((x + 3) % 4) * 4 + z),
            "z": (dp, x * 4 + (z + 3) % 4),
            "y": (((y + 3) % 4) * 2 + c, enc),
        }
        self.pos = {"x": x, "y": y, "z": z}
        self.partner = (y * 2 + (1 - c), enc)
        self.near = list(self.right.values()) + list(self.left.values()) + [self.partner]

    def column(self):
        steps = [(0, 1), (1, 0), (3, 0), (1, 1), (3, 1), (2, 0), (2, 1)]
        return [((self.y + dy) % 4, 1 - self.c if dc else self.c) for dy, dc in steps]

    def greet(self, others):
        sem = pltpu.get_barrier_semaphore()
        for other in others:
            pl.semaphore_signal(sem, inc=1, device_id=other, device_id_type=MESH)

    def meet(self, others):
        pl.semaphore_wait(pltpu.get_barrier_semaphore(), len(others))


class Copies:
    def __init__(self, send_sems, recv_sems):
        self.send_sems, self.recv_sems, self.used, self.started = send_sems, recv_sems, 0, []

    def start(self, src, dst, device):
        k = self.used
        self.used += 1
        copy = pltpu.make_async_remote_copy(
            src_ref=src,
            dst_ref=dst,
            send_sem=self.send_sems.at[k],
            recv_sem=self.recv_sems.at[k],
            device_id=device,
            device_id_type=MESH,
        )
        copy.start()
        self.started.append(copy)
        return copy

    def flush(self, some):
        for copy in some:
            copy.wait_send()
        gone = [id(copy) for copy in some]
        self.started = [copy for copy in self.started if id(copy) not in gone]

    def finish(self):
        self.flush(list(self.started))


class RingSum:
    def __init__(self, copies, place, axis, part, r1, r2):
        self.copies, self.part, self.r1, self.r2 = copies, part, r1, r2
        self.right, self.left = place.right[axis], place.left[axis]
        pos = place.pos[axis]
        self.pos, self.rt, self.lf, self.opp = pos, (pos + 1) % 4, (pos + 3) % 4, (pos + 2) % 4

    def send_opposite(self):
        self.a = self.copies.start(self.part(self.opp, 0), self.r1.at[0], self.right)
        self.b = self.copies.start(self.part(self.opp, 1), self.r1.at[1], self.left)

    def send_right(self):
        self.d = self.copies.start(self.part(self.rt, 1), self.r2.at[0, 1], self.right)

    def send_left(self):
        self.e = self.copies.start(self.part(self.lf, 0), self.r2.at[1, 0], self.left)

    def first(self):
        self.send_opposite()
        self.send_right()
        self.send_left()

    def second(self):
        self.a.wait_recv()
        mine = self.part(self.rt, 0)
        mine[...] = (mine[...].astype(F32) + self.r1[0].astype(F32)).astype(BF16)
        self.f = self.copies.start(mine, self.r2.at[0, 0], self.right)
        self.b.wait_recv()
        mine = self.part(self.lf, 1)
        mine[...] = (mine[...].astype(F32) + self.r1[1].astype(F32)).astype(BF16)
        self.g = self.copies.start(mine, self.r2.at[1, 1], self.left)

    def flush(self):
        self.copies.flush([self.a, self.b, self.d, self.e, self.f, self.g])

    def total(self):
        for copy in (self.d, self.e, self.f, self.g):
            copy.wait_recv()
        return [
            self.part(self.pos, h)[...].astype(F32)
            + self.r2[0, h].astype(F32)
            + self.r2[1, h].astype(F32)
            for h in (0, 1)
        ]


class RingGather:
    def __init__(self, copies, place, axis, block):
        self.copies, self.block = copies, block
        self.right, self.left = place.right[axis], place.left[axis]
        pos = place.pos[axis]
        self.pos, self.rt, self.lf = pos, (pos + 1) % 4, (pos + 3) % 4

    def first(self):
        own = self.block(self.pos, None)
        self.a = self.copies.start(own, own, self.right)
        self.b = self.copies.start(own, own, self.left)

    def second(self):
        self.a.wait_recv()
        part = self.block(self.lf, 0)
        self.d = self.copies.start(part, part, self.right)
        self.b.wait_recv()
        part = self.block(self.rt, 1)
        self.e = self.copies.start(part, part, self.left)

    def done(self):
        self.d.wait_recv()
        self.e.wait_recv()

    def flush(self):
        self.copies.flush([self.a, self.b, self.d, self.e])


HALVES = ((0, 128), (128, 256))


class PlaneSum:
    def __init__(self, copies, place, terms, sums, r1a, r2a, r1b, r2b):
        x, z = place.pos["x"], place.pos["z"]
        self.sums, self.place = sums, place

        def upper(b, h):
            return terms.at[b, 2 * h : 2 * h + 2, 0:128]

        def lower(b, h):
            return terms.at[2 * h : 2 * h + 2, b, 128:256]

        self.one = (
            RingSum(copies, place, "x", upper, r1a.at[0], r2a.at[0]),
            RingSum(copies, place, "z", lower, r1a.at[1], r2a.at[1]),
        )

        def upper_two(b, h):
            return sums.at[0, b, 64 * h : 64 * h + 64]

        def lower_two(b, h):
            return sums.at[1, b, 64 * h : 64 * h + 64]

        self.two = (
            RingSum(copies, place, "z", upper_two, r1b.at[0], r2b.at[0]),
            RingSum(copies, place, "x", lower_two, r1b.at[1], r2b.at[1]),
        )

    def step1(self):
        for ring in self.one:
            ring.first()

    def step2(self):
        for ring in self.one:
            ring.second()

    def step3(self):
        for k in (0, 1):
            low, high = self.one[k].total()
            self.sums[k, 0:2] = low.astype(BF16)
            self.sums[k, 2:4] = high.astype(BF16)
            self.two[k].first()

    def step4(self):
        for ring in self.one:
            ring.flush()
        for ring in self.two:
            ring.second()

    def finish(self, store):
        for k in (0, 1):
            low, high = self.two[k].total()
            store(k * 128, low.astype(BF16))
            store(k * 128 + 64, high.astype(BF16))


class PlaneGather:
    def __init__(self, copies, place, buf):
        x, z = place.pos["x"], place.pos["z"]
        half = buf.shape[2] // 2
        quarter = half // 2

        def upper(b, h):
            if h is None:
                return buf.at[b, z, 0:half]
            return buf.at[b, z, quarter * h : quarter * h + quarter]

        def lower(b, h):
            if h is None:
                return buf.at[x, b, half : 2 * half]
            return buf.at[x, b, half + quarter * h : half + quarter * h + quarter]

        def upper_two(b, h):
            if h is None:
                return buf.at[:, b, 0:half]
            return buf.at[2 * h : 2 * h + 2, b, 0:half]

        def lower_two(b, h):
            if h is None:
                return buf.at[b, :, half : 2 * half]
            return buf.at[b, 2 * h : 2 * h + 2, half : 2 * half]

        self.one = (
            RingGather(copies, place, "x", upper),
            RingGather(copies, place, "z", lower),
        )
        self.two = (
            RingGather(copies, place, "z", upper_two),
            RingGather(copies, place, "x", lower_two),
        )

    def step1(self):
        for ring in self.one:
            ring.first()

    def step2(self):
        for ring in self.one:
            ring.second()

    def step3(self):
        for one, two in zip(self.one, self.two):
            one.done()
            two.first()

    def step4(self):
        for ring in self.two:
            ring.second()

    def done(self):
        for ring in self.two:
            ring.done()


def layer_kernel(
    nbrs,
    blocks,
    hidden,
    encodings,
    cotangent,
    wk_hbm,
    wv_hbm,
    wq_hbm,
    wo_hbm,
    layer_hbm,
    grad_hidden_hbm,
    grad_encodings_hbm,
    grad_wq_hbm,
    grad_wk_hbm,
    grad_wv_hbm,
    grad_wo_hbm,
    weights,
    out_weight,
    terms,
    sums,
    r1a,
    r2a,
    r1b,
    r2b,
    pair,
    cots,
    encs,
    hids,
    queries,
    grads,
    prob,
    scored,
    flipped,
    spread_h,
    spread_v,
    theirs,
    side_t,
    dense_in,
    dense_sum,
    dense_r,
    part_r1,
    part_r2,
    rows_out,
    grads_out,
    load_sems,
    send_sems,
    recv_sems,
):
    place = Place()
    x, y, z, c = place.x, place.y, place.z, place.c
    copies = Copies(send_sems, recv_sems)
    column = place.column()
    met = place.near + [(oy * 2 + oc, place.enc) for oy, oc in column[3:]]
    loads = [
        pltpu.make_async_copy(src, dst, load_sems.at[k])
        for k, (src, dst) in enumerate(
            [
                (wk_hbm, weights.at[0]),
                (wv_hbm, weights.at[1]),
                (wq_hbm, weights.at[2]),
                (wo_hbm, out_weight),
            ]
        )
    ]
    for load in loads:
        load.start()
    place.greet(met)
    results = [
        pltpu.make_async_copy(src, dst, load_sems.at[4 + k])
        for k, (src, dst) in enumerate(
            [
                (rows_out.at[0], layer_hbm),
                (rows_out.at[1], grad_hidden_hbm),
                (rows_out.at[2], grad_encodings_hbm),
                (grads_out.at[0], grad_wq_hbm),
                (grads_out.at[0], grad_wk_hbm),
                (grads_out.at[1], grad_wv_hbm),
                (grads_out.at[1], grad_wo_hbm),
            ]
        )
    ]

    left = (encodings, encodings, hidden)
    keys, values, query, grad = [
        PlaneSum(
            copies, place, terms.at[k], sums.at[k], r1a.at[k], r2a.at[k], r1b.at[k], r2b.at[k]
        )
        for k in range(4)
    ]

    def make_terms(k):
        loads[k].wait()
        rows = left[k][...]

        def body(b, carry):
            product = mm(rows, weights[k, :, columns(b)]).astype(BF16)
            for i in range(4):
                terms[k, b, i] = product[:, i * 256 : i * 256 + 256]
            return carry

        lax.fori_loop(0, 4, body, 0)

    def make_grad_terms():
        loads[3].wait()
        rows = cotangent[...]

        def body(b, carry):
            for i in range(4):
                span = pl.ds(pl.multiple_of(b * 1024 + i * 256, 256), 256)
                product = lax.dot_general(rows, out_weight[span, :], NT, preferred_element_type=F32)
                terms[3, b, i] = product.astype(BF16)
            return carry

        lax.fori_loop(0, 4, body, 0)

    def columns(b):
        return pl.ds(pl.multiple_of(b * 1024, 1024), 1024)

    def row_block(ref):
        def block(b, h):
            if h is None:
                return ref.at[b, c]
            return ref.at[b, c, 128 * h : 128 * h + 128]

        return block

    def pair_block(k):
        def block(b, h):
            if h is None:
                return pair.at[k, b, c]
            return pair.at[k, b, c, h]

        return block

    gather_cots = RingGather(copies, place, "y", row_block(cots))
    gather_encs = RingGather(copies, place, "y", row_block(encs))
    gather_keys, gather_values = [
        RingGather(copies, place, "y", pair_block(k)) for k in (0, 1)
    ]

    def swap(gather, mine):
        gather.done()
        return copies.start(mine, mine, place.partner)

    def store_pair(k):
        def store(row, value):
            at = row % 128
            pair[k, y, c, row // 128, at : at + 64] = value

        return store

    def store_to(ref):
        def store(row, value):
            ref[row : row + 64] = value

        return store

    scale = HD ** (-0.5)
    cases = [(t, h) for t in range(4) for h in range(2)]

    def rows_of(ref, t, h):
        return ref[t * 64 : t * 64 + 64, h * 128 : h * 128 + 128]

    def picked(which, t, h):
        return jnp.concatenate(
            [
                pair[which, n // 4, (n // 2) % 2, n % 2, :, h * 128 : h * 128 + 128]
                for n in (nbrs[t, 0], nbrs[t, 1])
            ],
            axis=0,
        )

    def attend():
        slot = lax.broadcasted_iota(jnp.int32, (64, 256), 1)
        for i, (t, h) in enumerate(cases):
            limit0 = BLK * blocks[nbrs[t, 0]]
            limit1 = BLK * blocks[nbrs[t, 1]]
            valid = slot < jnp.where(slot < 128, limit0, limit1 + 128)
            scores = (
                lax.dot_general(
                    rows_of(queries, t, h), picked(0, t, h), NT, preferred_element_type=F32
                )
                * scale
            )
            scores = jnp.where(valid, scores, -1e30)
            top = jnp.max(scores, axis=1, keepdims=True)
            exps = jnp.where(valid, jnp.exp(scores - top), 0.0)
            total = jnp.sum(exps, axis=1, keepdims=True)
            output = mm(exps.astype(BF16), picked(1, t, h)) / total
            terms[0, x, z, t * 64 : t * 64 + 64, h * 128 : h * 128 + 128] = output.astype(BF16)
            prob[h, t * 64 : t * 64 + 64] = exps / total

    def attend_back():
        for t, h in cases:
            weight = prob[h, t * 64 : t * 64 + 64]
            grad_prob = lax.dot_general(
                rows_of(grads, t, h), picked(1, t, h), NT, preferred_element_type=F32
            )
            inner = jnp.sum(weight * grad_prob, axis=1, keepdims=True)
            found = weight * (grad_prob - inner) * scale
            scored[h, t * 64 : t * 64 + 64] = found
            term = mm(found.astype(BF16), picked(0, t, h))
            terms[1, x, z, t * 64 : t * 64 + 64, h * 128 : h * 128 + 128] = term.astype(BF16)

    def flip(source):
        for h in range(2):
            flipped[h] = source[h].T

    def neighbour_grads(which, rows):
        lane = lax.broadcasted_iota(jnp.int32, (128, 256), 1)
        names = []
        for j in range(2):
            name = jnp.where(lane < 64, nbrs[0, j], nbrs[1, j])
            name = jnp.where(lane < 128, name, nbrs[2, j])
            names.append(jnp.where(lane < 192, name, nbrs[3, j]))

        def body(i, carry):
            for h in range(2):
                first, second = flipped[h, 0:128], flipped[h, 128:256]
                chosen = jnp.concatenate(
                    [
                        jnp.where(
                            names[0] == n,
                            first,
                            jnp.where(names[1] == n, second, jnp.zeros_like(first)),
                        )
                        for n in (2 * i, 2 * i + 1)
                    ],
                    axis=0,
                ).astype(BF16)
                term = mm(chosen, rows[:, h * 128 : h * 128 + 128]).astype(BF16)
                for j in range(2):
                    pair[which, i // 2, i % 2, j, :, h * 128 : h * 128 + 128] = term[
                        j * 128 : j * 128 + 128
                    ]
            return carry

        lax.fori_loop(0, 8, body, 0)

    def swap_dense(k):
        return copies.start(pair.at[k, :, 1 - c], dense_in.at[k], place.partner)

    def send_dense(k, swapped):
        swapped.wait_recv()
        for b in range(4):
            dense_sum[b, k] = (pair[k, b, c].astype(F32) + dense_in[k, b].astype(F32)).astype(BF16)
        return [
            copies.start(
                dense_sum.at[(y + step) % 4, k],
                dense_r.at[i, k],
                (((y + step) % 4) * 2 + c, place.enc),
            )
            for i, step in enumerate((1, 3, 2))
        ]

    def sum_dense(k, moves):
        for move in moves:
            move.wait_recv()
        total = dense_sum[y, k].astype(F32)
        for i in range(3):
            total = total + dense_r[i, k].astype(F32)
        terms[2 + k, x, z] = total.astype(BF16).reshape(256, 256)

    net_h, net_q, net_k, net_v = [PlaneGather(copies, place, terms.at[k]) for k in range(4)]
    net_sh, net_sv = [PlaneGather(copies, place, ref) for ref in (spread_h, spread_v)]

    def swap_half(k):
        return copies.start(terms.at[k, :, pl.ds(2 * (1 - c), 2)], theirs.at[k - 1], place.partner)

    def ring_of(k):
        def part(b, h):
            return r2a.at[2 * (k - 1) + b // 2, b % 2, h]

        return RingSum(copies, place, "y", part, part_r1.at[k - 1], part_r2.at[k - 1])

    def weight_grad(k, ring):
        def block(b):
            own = jnp.concatenate([terms[k, b, 2 * c + i] for i in (0, 1)], axis=1)
            other = jnp.concatenate([theirs[k - 1, b, i] for i in (0, 1)], axis=1)
            both = jnp.concatenate([own, other], axis=0)
            product = mm(side_t[k - 1], both).astype(BF16)
            for h in (0, 1):
                for i in (0, 1):
                    quarter = product[256 * h : 256 * h + 256, 256 * i : 256 * i + 256]
                    r2a[2 * (k - 1) + b // 2, b % 2, h, i] = quarter.reshape(2, 128, 256)

        block(ring.opp)
        ring.send_opposite()
        block(ring.rt)
        ring.send_right()
        block(ring.lf)
        ring.send_left()
        block(ring.pos)

    def store_grad(k, ring):
        for h, found in enumerate(ring.total()):
            for i in (0, 1):
                grads_out[0, 256 * h : 256 * h + 256, 256 * i : 256 * i + 256] = found[i].reshape(
                    256, 256
                )
        results[2 + k].start()

    def wide(k, b):
        return jnp.concatenate([terms[k, b, i] for i in range(4)], axis=1)

    def accumulate(k, make):
        rows_out[k] = make(0)

        def body(b, carry):
            rows_out[k] += make(b)
            return carry

        lax.fori_loop(1, 4, body, 0)
        results[k].start()

    def transposed(k, slot, b):
        return lax.dot_general(
            wide(k, b), weights[slot, :, columns(b)], NT, preferred_element_type=F32
        )

    def turn(source, store):
        def body(t, carry):
            rows = []
            for e in (2 * t, 2 * t + 1):
                span = pl.ds(pl.multiple_of(e * 16, 16), 16)
                rows += [source[d // 2, d % 2, span] for d in range(8)]
            store(t, jnp.concatenate(rows, axis=0).T)
            return carry

        lax.fori_loop(0, 8, body, 0)

    def store_cots(t, found):
        for i in range(4):
            sums[t // 2, t % 2, i] = found[128 * i : 128 * i + 128]

    def store_encs(t, found):
        for i in range(4):
            r1a[t // 2, t % 2, i // 2, i % 2] = found[128 * i : 128 * i + 128]

    def exchange(k, spread):
        span = pl.ds(pl.multiple_of(place.enc * 16, 16), 16)
        moves = [
            copies.start(
                terms.at[k, oy, pl.ds(2 * oc, 2), span],
                spread.at[x, z, place.dp],
                (oy * 2 + oc, place.enc),
            )
            for oy, oc in column
        ]
        spread[x, z, place.dp] = terms[k, y, pl.ds(2 * c, 2), span]
        return moves

    def whole_grad(turned, spread):
        total = None
        for b in range(4):
            sides = jnp.concatenate(
                [
                    jnp.concatenate([turned(b, j, i) for j in (0, 1)], axis=1) for i in range(4)
                ],
                axis=0,
            )
            rows = jnp.concatenate(
                [
                    jnp.concatenate([spread[b, k, :, i].reshape(128, 256) for i in (0, 1)], axis=1)
                    for k in range(4)
                ],
                axis=0,
            )
            term = mm(sides, rows)
            total = term if total is None else total + term
        return total

    cots[y, c] = cotangent[...]
    encs[y, c] = encodings[...]
    hids[0] = hidden[...]
    make_terms(0)
    place.meet(met)
    keys.step1()
    gather_cots.first()
    swap_hids = copies.start(hids.at[0], hids.at[1], place.partner)
    make_terms(1)
    values.step1()
    gather_encs.first()
    make_terms(2)
    keys.step2()
    query.step1()
    values.step2()
    gather_cots.second()
    make_grad_terms()
    keys.step3()
    values.step3()
    grad.step1()
    keys.step4()
    gather_encs.second()
    query.step2()
    values.step4()
    keys.finish(store_pair(0))
    gather_keys.first()
    values.finish(store_pair(1))
    gather_values.first()
    swap_cots = swap(gather_cots, cots.at[:, c])
    swap_encs = swap(gather_encs, encs.at[:, c])
    query.step3()
    grad.step2()
    gather_keys.second()
    query.step4()
    gather_values.second()
    grad.step3()
    swap_keys = swap(gather_keys, pair.at[0, :, c])
    query.finish(store_to(queries))
    swap_values = swap(gather_values, pair.at[1, :, c])
    swap_keys.wait_recv()
    swap_values.wait_recv()
    attend()
    net_h.step1()
    grad.step4()
    flip(prob)
    net_h.step2()
    grad.finish(store_to(grads))
    attend_back()
    net_q.step1()
    net_h.step3()
    gather_keys.flush()
    gather_values.flush()
    copies.flush([swap_keys, swap_values])
    neighbour_grads(1, grads)
    swap_dense_v = swap_dense(1)
    flip(scored)
    neighbour_grads(0, queries)
    swap_dense_k = swap_dense(0)
    net_q.step2()
    moves_dv = send_dense(1, swap_dense_v)
    moves_dk = send_dense(0, swap_dense_k)
    net_q.step3()
    swap_hids.wait_recv()
    for k in (0, 1):
        side_t[0, :, k * 256 : k * 256 + 256] = hids[k].T
    net_h.step4()
    sum_dense(1, moves_dv)
    net_v.step1()
    sum_dense(0, moves_dk)
    net_k.step1()
    net_q.step4()
    net_v.step2()
    net_k.step2()
    net_h.done()
    moves_h = exchange(0, spread_h)
    net_v.step3()
    net_q.done()
    swap_q = swap_half(1)
    net_k.step3()
    ring_q, ring_k = ring_of(1), ring_of(2)
    swap_q.wait_recv()
    weight_grad(1, ring_q)
    for move in moves_h:
        move.wait_recv()
    net_sh.step1()
    swap_encs.wait_recv()
    side_t[1, :, 0:256] = encs[y, c].T
    side_t[1, :, 256:512] = encs[y, 1 - c].T
    net_v.step4()
    net_k.step4()
    net_sh.step2()
    accumulate(0, lambda b: mm(wide(0, b), out_weight[columns(b), :]))
    net_v.done()
    moves_v = exchange(3, spread_v)
    net_k.done()
    swap_k = swap_half(2)
    ring_q.second()
    for move in moves_v:
        move.wait_recv()
    net_sv.step1()
    net_sh.step3()
    swap_k.wait_recv()
    weight_grad(2, ring_k)
    net_sv.step2()
    swap_cots.wait_recv()
    for total in (keys, values, query, grad):
        for ring in total.two:
            ring.flush()
    turn(cots, store_cots)
    net_sv.step3()
    accumulate(1, lambda b: transposed(1, 2, b))
    net_sh.step4()
    turn(encs, store_encs)
    store_grad(1, ring_q)
    accumulate(2, lambda b: transposed(2, 0, b) + transposed(3, 1, b))
    net_sv.step4()
    net_sh.done()
    grads_out[1] = whole_grad(lambda b, j, i: sums[b, j, i], spread_h).T
    results[6].start()
    ring_k.second()
    net_sv.done()
    results[6].wait()
    grads_out[1] = whole_grad(lambda b, j, i: r1a[b, j, i // 2, i % 2], spread_v)
    results[5].start()
    results[3].wait()
    store_grad(2, ring_k)
    for k in (0, 1, 2, 4, 5):
        results[k].wait()
    copies.finish()


def copy_kernel(*refs):
    sems = refs[-1]
    count = (len(refs) - 1) // 3
    loads, moves = [], []
    for k in range(count):
        held = refs[2 * count + k]
        loads.append(pltpu.make_async_copy(refs[k], held, sems.at[0, k]))
        moves.append(pltpu.make_async_copy(held, refs[count + k], sems.at[1, k]))
    for load in loads:
        load.start()
    for load, move in zip(loads, moves):
        load.wait()
        move.start()
    for move in moves:
        move.wait()


def vmem():
    return pl.BlockSpec(memory_space=pltpu.VMEM)


def hbm():
    return pl.BlockSpec(memory_space=pl.ANY)


def shape(*dims, dtype=BF16):
    return jax.ShapeDtypeStruct(dims, dtype)


def per_device(
    hidden,
    encodings,
    query_weight,
    key_weight,
    value_weight,
    out_weight,
    out_cotangent,
    stretch_nbrs,
    nbr_blocks,
):
    flat_enc = encodings.reshape(256, 512)
    dma = pltpu.SemaphoreType.DMA
    limit = 62 * 1024 * 1024
    results = [shape(256, 512, dtype=F32)] * 3 + [shape(512, 512, dtype=F32)] * 4
    outs = pl.pallas_call(
        layer_kernel,
        out_shape=results,
        in_specs=[pl.BlockSpec(memory_space=pltpu.SMEM)] * 2 + [vmem()] * 3 + [hbm()] * 4,
        out_specs=[hbm()] * 7,
        scratch_shapes=[
            pltpu.VMEM((3, 512, 4096), BF16),
            pltpu.VMEM((4096, 512), BF16),
            pltpu.VMEM((4, 4, 4, 256, 256), BF16),
            pltpu.VMEM((4, 2, 4, 128, 256), BF16),
            pltpu.VMEM((4, 2, 2, 2, 128, 256), BF16),
            pltpu.VMEM((4, 2, 2, 2, 2, 128, 256), BF16),
            pltpu.VMEM((4, 2, 2, 64, 256), BF16),
            pltpu.VMEM((4, 2, 2, 2, 64, 256), BF16),
            pltpu.VMEM((2, 4, 2, 2, 128, 256), BF16),
            pltpu.VMEM((4, 2, 256, 512), BF16),
            pltpu.VMEM((4, 2, 256, 512), BF16),
            pltpu.VMEM((2, 256, 512), BF16),
            pltpu.VMEM((256, 256), BF16),
            pltpu.VMEM((256, 256), BF16),
            pltpu.VMEM((2, 256, 256), F32),
            pltpu.VMEM((2, 256, 256), F32),
            pltpu.VMEM((2, 256, 256), F32),
            pltpu.VMEM((4, 4, 8, 2, 16, 256), BF16),
            pltpu.VMEM((4, 4, 8, 2, 16, 256), BF16),
            pltpu.VMEM((2, 4, 2, 256, 256), BF16),
            pltpu.VMEM((2, 512, 512), BF16),
            pltpu.VMEM((2, 4, 2, 128, 256), BF16),
            pltpu.VMEM((4, 2, 2, 128, 256), BF16),
            pltpu.VMEM((3, 2, 2, 128, 256), BF16),
            pltpu.VMEM((2, 2, 2, 2, 128, 256), BF16),
            pltpu.VMEM((2, 2, 2, 2, 2, 128, 256), BF16),
            pltpu.VMEM((3, 256, 512), F32),
            pltpu.VMEM((2, 512, 512), F32),
            dma((11,)),
            dma((256,)),
            dma((256,)),
        ],
        compiler_params=pltpu.CompilerParams(
            collective_id=0, has_side_effects=True, vmem_limit_bytes=limit
        ),
    )(
        stretch_nbrs,
        nbr_blocks,
        hidden,
        flat_enc,
        out_cotangent,
        key_weight,
        value_weight,
        query_weight,
        out_weight,
    )
    outs = pl.pallas_call(
        copy_kernel,
        out_shape=results,
        in_specs=[hbm()] * 7,
        out_specs=[hbm()] * 7,
        scratch_shapes=[pltpu.VMEM(r.shape, F32) for r in results] + [dma((2, 7))],
        compiler_params=pltpu.CompilerParams(vmem_limit_bytes=limit),
    )(*outs)
    layer_out, grad_hidden, grad_enc, grad_wq, grad_wk, grad_wv, grad_wo = outs
    return (
        layer_out,
        grad_hidden,
        grad_enc.reshape(encodings.shape),
        grad_wq,
        grad_wk,
        grad_wv,
        grad_wo,
    )


def solution(mesh):
    in_specs = (
        P("dp", "enc"),
        P("dp", None, "enc"),
        P("enc", None),
        P("enc", None),
        P("enc", None),
        P(None, "enc"),
        P("dp", "enc"),
        P("dp", None),
        P(),
    )
    out_specs = (
        P("dp", "enc"),
        P("dp", "enc"),
        P("dp", None, "enc"),
        P("enc", "dp"),
        P("enc", "dp"),
        P("enc", "dp"),
        P("dp", "enc"),
    )
    return jax.shard_map(
        per_device, mesh=mesh, in_specs=in_specs, out_specs=out_specs, check_vma=False
    )
```

```python
import functools

import jax
import jax.numpy as jnp
from jax import lax
from jax.experimental import pallas as pl
from jax.experimental.pallas import tpu as pltpu
from jax.sharding import PartitionSpec as P

HD = 128
BLK = 16
MESH = pl.DeviceIdType.MESH
F32 = jnp.float32
BF16 = jnp.bfloat16
NT = (((1,), (1,)), ((), ()))
TN = (((0,), (0,)), ((), ()))


def mm(a, b):
    return jnp.dot(a, b, preferred_element_type=F32)


class Place:
    def __init__(self):
        self.dp = lax.axis_index("dp")
        self.enc = lax.axis_index("enc")
        dp, enc = self.dp, self.enc
        self.y, self.c = dp // 2, dp % 2
        self.x, self.z = enc // 4, enc % 4
        x, y, z, c = self.x, self.y, self.z, self.c
        self.right = {
            "x": (dp, ((x + 1) % 4) * 4 + z),
            "z": (dp, x * 4 + (z + 1) % 4),
            "y": (((y + 1) % 4) * 2 + c, enc),
        }
        self.left = {
            "x": (dp, ((x + 3) % 4) * 4 + z),
            "z": (dp, x * 4 + (z + 3) % 4),
            "y": (((y + 3) % 4) * 2 + c, enc),
        }
        self.pos = {"x": x, "y": y, "z": z}
        self.partner = (y * 2 + (1 - c), enc)
        self.near = list(self.right.values()) + list(self.left.values()) + [self.partner]

    def column(self):
        steps = [(0, 1), (1, 0), (3, 0), (1, 1), (3, 1), (2, 0), (2, 1)]
        return [((self.y + dy) % 4, 1 - self.c if dc else self.c) for dy, dc in steps]

    def greet(self, others):
        sem = pltpu.get_barrier_semaphore()
        for other in others:
            pl.semaphore_signal(sem, inc=1, device_id=other, device_id_type=MESH)

    def meet(self, others):
        pl.semaphore_wait(pltpu.get_barrier_semaphore(), len(others))


class Copies:
    def __init__(self, send_sems, recv_sems):
        self.send_sems, self.recv_sems, self.used, self.started = send_sems, recv_sems, 0, []

    def start(self, src, dst, device):
        k = self.used
        self.used += 1
        copy = pltpu.make_async_remote_copy(
            src_ref=src,
            dst_ref=dst,
            send_sem=self.send_sems.at[k],
            recv_sem=self.recv_sems.at[k],
            device_id=device,
            device_id_type=MESH,
        )
        copy.start()
        self.started.append(copy)
        return copy

    def flush(self, some):
        for copy in some:
            copy.wait_send()
        gone = [id(copy) for copy in some]
        self.started = [copy for copy in self.started if id(copy) not in gone]

    def finish(self):
        self.flush(list(self.started))


class RingSum:
    def __init__(self, copies, place, axis, part, r1, r2):
        self.copies, self.part, self.r1, self.r2 = copies, part, r1, r2
        self.right, self.left = place.right[axis], place.left[axis]
        pos = place.pos[axis]
        self.pos, self.rt, self.lf, self.opp = pos, (pos + 1) % 4, (pos + 3) % 4, (pos + 2) % 4

    def send_opposite(self):
        self.a = self.copies.start(self.part(self.opp, 0), self.r1.at[0], self.right)
        self.b = self.copies.start(self.part(self.opp, 1), self.r1.at[1], self.left)

    def send_right(self):
        self.d = self.copies.start(self.part(self.rt, 1), self.r2.at[0, 1], self.right)

    def send_left(self):
        self.e = self.copies.start(self.part(self.lf, 0), self.r2.at[1, 0], self.left)

    def first(self):
        self.send_opposite()
        self.send_right()
        self.send_left()

    def second(self):
        self.a.wait_recv()
        mine = self.part(self.rt, 0)
        mine[...] = (mine[...].astype(F32) + self.r1[0].astype(F32)).astype(BF16)
        self.f = self.copies.start(mine, self.r2.at[0, 0], self.right)
        self.b.wait_recv()
        mine = self.part(self.lf, 1)
        mine[...] = (mine[...].astype(F32) + self.r1[1].astype(F32)).astype(BF16)
        self.g = self.copies.start(mine, self.r2.at[1, 1], self.left)

    def flush(self):
        self.copies.flush([self.a, self.b, self.d, self.e, self.f, self.g])

    def total(self):
        for copy in (self.d, self.e, self.f, self.g):
            copy.wait_recv()
        return [
            self.part(self.pos, h)[...].astype(F32)
            + self.r2[0, h].astype(F32)
            + self.r2[1, h].astype(F32)
            for h in (0, 1)
        ]


class RingGather:
    def __init__(self, copies, place, axis, block):
        self.copies, self.block = copies, block
        self.right, self.left = place.right[axis], place.left[axis]
        pos = place.pos[axis]
        self.pos, self.rt, self.lf = pos, (pos + 1) % 4, (pos + 3) % 4

    def first(self):
        own = self.block(self.pos, None)
        self.a = self.copies.start(own, own, self.right)
        self.b = self.copies.start(own, own, self.left)

    def second(self):
        self.a.wait_recv()
        part = self.block(self.lf, 0)
        self.d = self.copies.start(part, part, self.right)
        self.b.wait_recv()
        part = self.block(self.rt, 1)
        self.e = self.copies.start(part, part, self.left)

    def done(self):
        self.d.wait_recv()
        self.e.wait_recv()

    def flush(self):
        self.copies.flush([self.a, self.b, self.d, self.e])


HALVES = ((0, 128), (128, 256))


class PlaneSum:
    def __init__(self, copies, place, terms, sums, r1a, r2a, r1b, r2b):
        x, z = place.pos["x"], place.pos["z"]
        self.sums, self.place = sums, place

        def upper(b, h):
            return terms.at[b, 2 * h : 2 * h + 2, 0:128]

        def lower(b, h):
            return terms.at[2 * h : 2 * h + 2, b, 128:256]

        self.one = (
            RingSum(copies, place, "x", upper, r1a.at[0], r2a.at[0]),
            RingSum(copies, place, "z", lower, r1a.at[1], r2a.at[1]),
        )

        def upper_two(b, h):
            return sums.at[0, b, 64 * h : 64 * h + 64]

        def lower_two(b, h):
            return sums.at[1, b, 64 * h : 64 * h + 64]

        self.two = (
            RingSum(copies, place, "z", upper_two, r1b.at[0], r2b.at[0]),
            RingSum(copies, place, "x", lower_two, r1b.at[1], r2b.at[1]),
        )

    def step1(self):
        for ring in self.one:
            ring.first()

    def step2(self):
        for ring in self.one:
            ring.second()

    def step3(self):
        for k in (0, 1):
            low, high = self.one[k].total()
            self.sums[k, 0:2] = low.astype(BF16)
            self.sums[k, 2:4] = high.astype(BF16)
            self.two[k].first()

    def step4(self):
        for ring in self.one:
            ring.flush()
        for ring in self.two:
            ring.second()

    def finish(self, store):
        for k in (0, 1):
            low, high = self.two[k].total()
            store(k * 128, low.astype(BF16))
            store(k * 128 + 64, high.astype(BF16))


class PlaneGather:
    def __init__(self, copies, place, buf):
        x, z = place.pos["x"], place.pos["z"]
        half = buf.shape[2] // 2
        quarter = half // 2

        def upper(b, h):
            if h is None:
                return buf.at[b, z, 0:half]
            return buf.at[b, z, quarter * h : quarter * h + quarter]

        def lower(b, h):
            if h is None:
                return buf.at[x, b, half : 2 * half]
            return buf.at[x, b, half + quarter * h : half + quarter * h + quarter]

        def upper_two(b, h):
            if h is None:
                return buf.at[:, b, 0:half]
            return buf.at[2 * h : 2 * h + 2, b, 0:half]

        def lower_two(b, h):
            if h is None:
                return buf.at[b, :, half : 2 * half]
            return buf.at[b, 2 * h : 2 * h + 2, half : 2 * half]

        self.one = (
            RingGather(copies, place, "x", upper),
            RingGather(copies, place, "z", lower),
        )
        self.two = (
            RingGather(copies, place, "z", upper_two),
            RingGather(copies, place, "x", lower_two),
        )

    def step1(self):
        for ring in self.one:
            ring.first()

    def step2(self):
        for ring in self.one:
            ring.second()

    def step3(self):
        for one, two in zip(self.one, self.two):
            one.done()
            two.first()

    def step4(self):
        for ring in self.two:
            ring.second()

    def done(self):
        for ring in self.two:
            ring.done()


def layer_kernel(
    nbrs,
    blocks,
    hidden,
    encodings,
    cotangent,
    wk_hbm,
    wv_hbm,
    wq_hbm,
    wo_hbm,
    layer_hbm,
    grad_hidden_hbm,
    grad_encodings_hbm,
    grad_wq_hbm,
    grad_wk_hbm,
    grad_wv_hbm,
    grad_wo_hbm,
    weights,
    out_weight,
    terms,
    sums,
    r1a,
    r2a,
    r1b,
    r2b,
    pair,
    cots,
    encs,
    hids,
    queries,
    grads,
    prob,
    scored,
    flipped,
    spread_h,
    spread_v,
    theirs,
    side_t,
    dense_in,
    dense_sum,
    dense_r,
    part_r1,
    part_r2,
    rows_out,
    grads_out,
    load_sems,
    send_sems,
    recv_sems,
):
    place = Place()
    x, y, z, c = place.x, place.y, place.z, place.c
    copies = Copies(send_sems, recv_sems)
    column = place.column()
    met = place.near + [(oy * 2 + oc, place.enc) for oy, oc in column[3:]]
    loads = [
        pltpu.make_async_copy(src, dst, load_sems.at[k])
        for k, (src, dst) in enumerate(
            [
                (wk_hbm, weights.at[0]),
                (wv_hbm, weights.at[1]),
                (wq_hbm, weights.at[2]),
                (wo_hbm, out_weight),
            ]
        )
    ]
    for load in loads:
        load.start()
    place.greet(met)
    results = [
        pltpu.make_async_copy(src, dst, load_sems.at[4 + k])
        for k, (src, dst) in enumerate(
            [
                (rows_out.at[0], layer_hbm),
                (rows_out.at[1], grad_hidden_hbm),
                (rows_out.at[2], grad_encodings_hbm),
                (grads_out.at[0], grad_wq_hbm),
                (grads_out.at[0], grad_wk_hbm),
                (grads_out.at[1], grad_wv_hbm),
                (grads_out.at[1], grad_wo_hbm),
            ]
        )
    ]

    left = (encodings, encodings, hidden)
    keys, values, query, grad = [
        PlaneSum(
            copies, place, terms.at[k], sums.at[k], r1a.at[k], r2a.at[k], r1b.at[k], r2b.at[k]
        )
        for k in range(4)
    ]

    def make_terms(k):
        loads[k].wait()
        rows = left[k][...]

        def body(b, carry):
            product = mm(rows, weights[k, :, columns(b)]).astype(BF16)
            for i in range(4):
                terms[k, b, i] = product[:, i * 256 : i * 256 + 256]
            return carry

        lax.fori_loop(0, 4, body, 0)

    def make_grad_terms():
        loads[3].wait()
        rows = cotangent[...]

        def body(b, carry):
            for i in range(4):
                span = pl.ds(pl.multiple_of(b * 1024 + i * 256, 256), 256)
                product = lax.dot_general(rows, out_weight[span, :], NT, preferred_element_type=F32)
                terms[3, b, i] = product.astype(BF16)
            return carry

        lax.fori_loop(0, 4, body, 0)

    def columns(b):
        return pl.ds(pl.multiple_of(b * 1024, 1024), 1024)

    def row_block(ref):
        def block(b, h):
            if h is None:
                return ref.at[b, c]
            return ref.at[b, c, 128 * h : 128 * h + 128]

        return block

    def pair_block(k):
        def block(b, h):
            if h is None:
                return pair.at[k, b, c]
            return pair.at[k, b, c, h]

        return block

    gather_cots = RingGather(copies, place, "y", row_block(cots))
    gather_encs = RingGather(copies, place, "y", row_block(encs))
    gather_keys, gather_values = [
        RingGather(copies, place, "y", pair_block(k)) for k in (0, 1)
    ]

    def swap(gather, mine):
        gather.done()
        return copies.start(mine, mine, place.partner)

    def store_pair(k):
        def store(row, value):
            at = row % 128
            pair[k, y, c, row // 128, at : at + 64] = value

        return store

    def store_to(ref):
        def store(row, value):
            ref[row : row + 64] = value

        return store

    scale = HD ** (-0.5)
    cases = [(t, h) for t in range(4) for h in range(2)]

    def rows_of(ref, t, h):
        return ref[t * 64 : t * 64 + 64, h * 128 : h * 128 + 128]

    def picked(which, t, h):
        return jnp.concatenate(
            [
                pair[which, n // 4, (n // 2) % 2, n % 2, :, h * 128 : h * 128 + 128]
                for n in (nbrs[t, 0], nbrs[t, 1])
            ],
            axis=0,
        )

    def attend():
        slot = lax.broadcasted_iota(jnp.int32, (64, 256), 1)
        for i, (t, h) in enumerate(cases):
            limit0 = BLK * blocks[nbrs[t, 0]]
            limit1 = BLK * blocks[nbrs[t, 1]]
            valid = slot < jnp.where(slot < 128, limit0, limit1 + 128)
            scores = (
                lax.dot_general(
                    rows_of(queries, t, h), picked(0, t, h), NT, preferred_element_type=F32
                )
                * scale
            )
            scores = jnp.where(valid, scores, -1e30)
            top = jnp.max(scores, axis=1, keepdims=True)
            exps = jnp.where(valid, jnp.exp(scores - top), 0.0)
            total = jnp.sum(exps, axis=1, keepdims=True)
            output = mm(exps.astype(BF16), picked(1, t, h)) / total
            terms[0, x, z, t * 64 : t * 64 + 64, h * 128 : h * 128 + 128] = output.astype(BF16)
            prob[h, t * 64 : t * 64 + 64] = exps / total

    def attend_back():
        for t, h in cases:
            weight = prob[h, t * 64 : t * 64 + 64]
            grad_prob = lax.dot_general(
                rows_of(grads, t, h), picked(1, t, h), NT, preferred_element_type=F32
            )
            inner = jnp.sum(weight * grad_prob, axis=1, keepdims=True)
            found = weight * (grad_prob - inner) * scale
            scored[h, t * 64 : t * 64 + 64] = found
            term = mm(found.astype(BF16), picked(0, t, h))
            terms[1, x, z, t * 64 : t * 64 + 64, h * 128 : h * 128 + 128] = term.astype(BF16)

    def flip(source):
        for h in range(2):
            flipped[h] = source[h].T

    def neighbour_grads(which, rows):
        lane = lax.broadcasted_iota(jnp.int32, (128, 256), 1)
        names = []
        for j in range(2):
            name = jnp.where(lane < 64, nbrs[0, j], nbrs[1, j])
            name = jnp.where(lane < 128, name, nbrs[2, j])
            names.append(jnp.where(lane < 192, name, nbrs[3, j]))

        def body(i, carry):
            for h in range(2):
                first, second = flipped[h, 0:128], flipped[h, 128:256]
                chosen = jnp.concatenate(
                    [
                        jnp.where(
                            names[0] == n,
                            first,
                            jnp.where(names[1] == n, second, jnp.zeros_like(first)),
                        )
                        for n in (2 * i, 2 * i + 1)
                    ],
                    axis=0,
                ).astype(BF16)
                term = mm(chosen, rows[:, h * 128 : h * 128 + 128]).astype(BF16)
                for j in range(2):
                    pair[which, i // 2, i % 2, j, :, h * 128 : h * 128 + 128] = term[
                        j * 128 : j * 128 + 128
                    ]
            return carry

        lax.fori_loop(0, 8, body, 0)

    def swap_dense(k):
        return copies.start(pair.at[k, :, 1 - c], dense_in.at[k], place.partner)

    def send_dense(k, swapped):
        swapped.wait_recv()
        for b in range(4):
            dense_sum[b, k] = (pair[k, b, c].astype(F32) + dense_in[k, b].astype(F32)).astype(BF16)
        return [
            copies.start(
                dense_sum.at[(y + step) % 4, k],
                dense_r.at[i, k],
                (((y + step) % 4) * 2 + c, place.enc),
            )
            for i, step in enumerate((1, 3, 2))
        ]

    def sum_dense(k, moves):
        for move in moves:
            move.wait_recv()
        total = dense_sum[y, k].astype(F32)
        for i in range(3):
            total = total + dense_r[i, k].astype(F32)
        terms[2 + k, x, z] = total.astype(BF16).reshape(256, 256)

    net_h, net_q, net_k, net_v = [PlaneGather(copies, place, terms.at[k]) for k in range(4)]
    net_sh, net_sv = [PlaneGather(copies, place, ref) for ref in (spread_h, spread_v)]

    def swap_half(k):
        return copies.start(terms.at[k, :, pl.ds(2 * (1 - c), 2)], theirs.at[k - 1], place.partner)

    def ring_of(k):
        def part(b, h):
            return r2a.at[2 * (k - 1) + b // 2, b % 2, h]

        return RingSum(copies, place, "y", part, part_r1.at[k - 1], part_r2.at[k - 1])

    def weight_grad(k, ring):
        def block(b):
            own = jnp.concatenate([terms[k, b, 2 * c + i] for i in (0, 1)], axis=1)
            other = jnp.concatenate([theirs[k - 1, b, i] for i in (0, 1)], axis=1)
            both = jnp.concatenate([own, other], axis=0)
            product = mm(side_t[k - 1], both).astype(BF16)
            for h in (0, 1):
                for i in (0, 1):
                    quarter = product[256 * h : 256 * h + 256, 256 * i : 256 * i + 256]
                    r2a[2 * (k - 1) + b // 2, b % 2, h, i] = quarter.reshape(2, 128, 256)

        block(ring.opp)
        ring.send_opposite()
        block(ring.rt)
        ring.send_right()
        block(ring.lf)
        ring.send_left()
        block(ring.pos)

    def store_grad(k, ring):
        for h, found in enumerate(ring.total()):
            for i in (0, 1):
                grads_out[0, 256 * h : 256 * h + 256, 256 * i : 256 * i + 256] = found[i].reshape(
                    256, 256
                )
        results[2 + k].start()

    def wide(k, b):
        return jnp.concatenate([terms[k, b, i] for i in range(4)], axis=1)

    def accumulate(k, make):
        rows_out[k] = make(0)

        def body(b, carry):
            rows_out[k] += make(b)
            return carry

        lax.fori_loop(1, 4, body, 0)
        results[k].start()

    def transposed(k, slot, b):
        return lax.dot_general(
            wide(k, b), weights[slot, :, columns(b)], NT, preferred_element_type=F32
        )

    def turn(source, store):
        def body(t, carry):
            rows = []
            for e in (2 * t, 2 * t + 1):
                span = pl.ds(pl.multiple_of(e * 16, 16), 16)
                rows += [source[d // 2, d % 2, span] for d in range(8)]
            store(t, jnp.concatenate(rows, axis=0).T)
            return carry

        lax.fori_loop(0, 8, body, 0)

    def store_cots(t, found):
        for i in range(4):
            sums[t // 2, t % 2, i] = found[128 * i : 128 * i + 128]

    def store_encs(t, found):
        for i in range(4):
            r1a[t // 2, t % 2, i // 2, i % 2] = found[128 * i : 128 * i + 128]

    def exchange(k, spread):
        span = pl.ds(pl.multiple_of(place.enc * 16, 16), 16)
        moves = [
            copies.start(
                terms.at[k, oy, pl.ds(2 * oc, 2), span],
                spread.at[x, z, place.dp],
                (oy * 2 + oc, place.enc),
            )
            for oy, oc in column
        ]
        spread[x, z, place.dp] = terms[k, y, pl.ds(2 * c, 2), span]
        return moves

    def whole_grad(turned, spread):
        total = None
        for b in range(4):
            sides = jnp.concatenate(
                [
                    jnp.concatenate([turned(b, j, i) for j in (0, 1)], axis=1) for i in range(4)
                ],
                axis=0,
            )
            rows = jnp.concatenate(
                [
                    jnp.concatenate([spread[b, k, :, i].reshape(128, 256) for i in (0, 1)], axis=1)
                    for k in range(4)
                ],
                axis=0,
            )
            term = mm(sides, rows)
            total = term if total is None else total + term
        return total

    cots[y, c] = cotangent[...]
    encs[y, c] = encodings[...]
    hids[0] = hidden[...]
    ring_q, ring_k = ring_of(1), ring_of(2)
    make_terms(0)
    place.meet(met)
    keys.step1()
    make_terms(1)
    keys.step2()
    gather_encs.first()
    values.step1()
    make_terms(2)
    keys.step3()
    values.step2()
    keys.step4()
    query.step1()
    keys.finish(store_pair(0))
    gather_keys.first()
    make_grad_terms()
    values.step3()
    query.step2()
    values.step4()
    grad.step1()
    values.finish(store_pair(1))
    gather_values.first()
    grad.step2()
    gather_keys.second()
    query.step3()
    gather_values.second()
    swap_keys = swap(gather_keys, pair.at[0, :, c])
    grad.step3()
    swap_values = swap(gather_values, pair.at[1, :, c])
    query.step4()
    gather_cots.first()
    grad.step4()
    query.finish(store_to(queries))
    swap_keys.wait_recv()
    swap_values.wait_recv()
    attend()
    net_h.step1()
    grad.finish(store_to(grads))
    attend_back()
    net_q.step1()
    gather_keys.flush()
    gather_values.flush()
    copies.flush([swap_keys, swap_values])
    net_h.step2()
    flip(prob)
    neighbour_grads(1, grads)
    swap_dense_v = swap_dense(1)
    swap_hids = copies.start(hids.at[0], hids.at[1], place.partner)
    net_q.step2()
    gather_encs.second()
    net_h.step3()
    moves_dv = send_dense(1, swap_dense_v)
    net_q.step3()
    flip(scored)
    neighbour_grads(0, queries)
    swap_dense_k = swap_dense(0)
    sum_dense(1, moves_dv)
    moves_dk = send_dense(0, swap_dense_k)
    net_v.step1()
    net_h.step4()
    net_v.step2()
    sum_dense(0, moves_dk)
    net_k.step1()
    swap_hids.wait_recv()
    for k in (0, 1):
        side_t[0, :, k * 256 : k * 256 + 256] = hids[k].T
    net_q.step4()
    net_h.done()
    net_k.step2()
    for total in (keys, values, query, grad):
        for ring in total.two:
            ring.flush()
    net_v.step3()
    moves_h = exchange(0, spread_h)
    net_q.done()
    swap_q = swap_half(1)
    swap_encs = swap(gather_encs, encs.at[:, c])
    net_k.step3()
    swap_q.wait_recv()
    weight_grad(1, ring_q)
    net_v.step4()
    net_k.step4()
    net_v.done()
    for move in moves_h:
        move.wait_recv()
    net_sh.step1()
    moves_v = exchange(3, spread_v)
    gather_cots.second()
    accumulate(0, lambda b: mm(wide(0, b), out_weight[columns(b), :]))
    net_k.done()
    ring_q.second()
    for move in moves_v:
        move.wait_recv()
    net_sv.step1()
    swap_encs.wait_recv()
    side_t[1, :, 0:256] = encs[y, c].T
    side_t[1, :, 256:512] = encs[y, 1 - c].T
    net_sh.step2()
    swap_k = swap_half(2)
    net_sv.step2()
    net_sh.step3()
    swap_k.wait_recv()
    weight_grad(2, ring_k)
    net_sv.step3()
    turn(encs, store_encs)
    net_sh.step4()
    swap_cots = swap(gather_cots, cots.at[:, c])
    accumulate(2, lambda b: transposed(2, 0, b) + transposed(3, 1, b))
    swap_cots.wait_recv()
    turn(cots, store_cots)
    ring_k.second()
    net_sv.step4()
    accumulate(1, lambda b: transposed(1, 2, b))
    store_grad(1, ring_q)
    net_sh.done()
    grads_out[1] = whole_grad(lambda b, j, i: sums[b, j, i], spread_h).T
    results[6].start()
    net_sv.done()
    results[6].wait()
    grads_out[1] = whole_grad(lambda b, j, i: r1a[b, j, i // 2, i % 2], spread_v)
    results[5].start()
    results[3].wait()
    store_grad(2, ring_k)
    for k in (0, 1, 2, 4, 5):
        results[k].wait()
    copies.finish()


def copy_kernel(*refs):
    sems = refs[-1]
    count = (len(refs) - 1) // 3
    loads, moves = [], []
    for k in range(count):
        held = refs[2 * count + k]
        loads.append(pltpu.make_async_copy(refs[k], held, sems.at[0, k]))
        moves.append(pltpu.make_async_copy(held, refs[count + k], sems.at[1, k]))
    for load in loads:
        load.start()
    for load, move in zip(loads, moves):
        load.wait()
        move.start()
    for move in moves:
        move.wait()


def vmem():
    return pl.BlockSpec(memory_space=pltpu.VMEM)


def hbm():
    return pl.BlockSpec(memory_space=pl.ANY)


def shape(*dims, dtype=BF16):
    return jax.ShapeDtypeStruct(dims, dtype)


def per_device(
    hidden,
    encodings,
    query_weight,
    key_weight,
    value_weight,
    out_weight,
    out_cotangent,
    stretch_nbrs,
    nbr_blocks,
):
    flat_enc = encodings.reshape(256, 512)
    dma = pltpu.SemaphoreType.DMA
    limit = 62 * 1024 * 1024
    results = [shape(256, 512, dtype=F32)] * 3 + [shape(512, 512, dtype=F32)] * 4
    outs = pl.pallas_call(
        layer_kernel,
        out_shape=results,
        in_specs=[pl.BlockSpec(memory_space=pltpu.SMEM)] * 2 + [vmem()] * 3 + [hbm()] * 4,
        out_specs=[hbm()] * 7,
        scratch_shapes=[
            pltpu.VMEM((3, 512, 4096), BF16),
            pltpu.VMEM((4096, 512), BF16),
            pltpu.VMEM((4, 4, 4, 256, 256), BF16),
            pltpu.VMEM((4, 2, 4, 128, 256), BF16),
            pltpu.VMEM((4, 2, 2, 2, 128, 256), BF16),
            pltpu.VMEM((4, 2, 2, 2, 2, 128, 256), BF16),
            pltpu.VMEM((4, 2, 2, 64, 256), BF16),
            pltpu.VMEM((4, 2, 2, 2, 64, 256), BF16),
            pltpu.VMEM((2, 4, 2, 2, 128, 256), BF16),
            pltpu.VMEM((4, 2, 256, 512), BF16),
            pltpu.VMEM((4, 2, 256, 512), BF16),
            pltpu.VMEM((2, 256, 512), BF16),
            pltpu.VMEM((256, 256), BF16),
            pltpu.VMEM((256, 256), BF16),
            pltpu.VMEM((2, 256, 256), F32),
            pltpu.VMEM((2, 256, 256), F32),
            pltpu.VMEM((2, 256, 256), F32),
            pltpu.VMEM((4, 4, 8, 2, 16, 256), BF16),
            pltpu.VMEM((4, 4, 8, 2, 16, 256), BF16),
            pltpu.VMEM((2, 4, 2, 256, 256), BF16),
            pltpu.VMEM((2, 512, 512), BF16),
            pltpu.VMEM((2, 4, 2, 128, 256), BF16),
            pltpu.VMEM((4, 2, 2, 128, 256), BF16),
            pltpu.VMEM((3, 2, 2, 128, 256), BF16),
            pltpu.VMEM((2, 2, 2, 2, 128, 256), BF16),
            pltpu.VMEM((2, 2, 2, 2, 2, 128, 256), BF16),
            pltpu.VMEM((3, 256, 512), F32),
            pltpu.VMEM((2, 512, 512), F32),
            dma((11,)),
            dma((256,)),
            dma((256,)),
        ],
        compiler_params=pltpu.CompilerParams(
            collective_id=0, has_side_effects=True, vmem_limit_bytes=limit
        ),
    )(
        stretch_nbrs,
        nbr_blocks,
        hidden,
        flat_enc,
        out_cotangent,
        key_weight,
        value_weight,
        query_weight,
        out_weight,
    )
    outs = pl.pallas_call(
        copy_kernel,
        out_shape=results,
        in_specs=[hbm()] * 7,
        out_specs=[hbm()] * 7,
        scratch_shapes=[pltpu.VMEM(r.shape, F32) for r in results] + [dma((2, 7))],
        compiler_params=pltpu.CompilerParams(vmem_limit_bytes=limit),
    )(*outs)
    layer_out, grad_hidden, grad_enc, grad_wq, grad_wk, grad_wv, grad_wo = outs
    return (
        layer_out,
        grad_hidden,
        grad_enc.reshape(encodings.shape),
        grad_wq,
        grad_wk,
        grad_wv,
        grad_wo,
    )


def solution(mesh):
    in_specs = (
        P("dp", "enc"),
        P("dp", None, "enc"),
        P("enc", None),
        P("enc", None),
        P("enc", None),
        P(None, "enc"),
        P("dp", "enc"),
        P("dp", None),
        P(),
    )
    out_specs = (
        P("dp", "enc"),
        P("dp", "enc"),
        P("dp", None, "enc"),
        P("enc", "dp"),
        P("enc", "dp"),
        P("enc", "dp"),
        P("dp", "enc"),
    )
    return jax.shard_map(
        per_device, mesh=mesh, in_specs=in_specs, out_specs=out_specs, check_vma=False
    )
```

```python
import functools

import jax
import jax.numpy as jnp
from jax import lax
from jax.experimental import pallas as pl
from jax.experimental.pallas import tpu as pltpu
from jax.sharding import PartitionSpec as P

HD = 128
BLK = 16
MESH = pl.DeviceIdType.MESH
F32 = jnp.float32
BF16 = jnp.bfloat16
NT = (((1,), (1,)), ((), ()))
TN = (((0,), (0,)), ((), ()))


def mm(a, b):
    return jnp.dot(a, b, preferred_element_type=F32)


class Place:
    def __init__(self):
        self.dp = lax.axis_index("dp")
        self.enc = lax.axis_index("enc")
        dp, enc = self.dp, self.enc
        self.y, self.c = dp // 2, dp % 2
        self.x, self.z = enc // 4, enc % 4
        x, y, z, c = self.x, self.y, self.z, self.c
        self.right = {
            "x": (dp, ((x + 1) % 4) * 4 + z),
            "z": (dp, x * 4 + (z + 1) % 4),
            "y": (((y + 1) % 4) * 2 + c, enc),
        }
        self.left = {
            "x": (dp, ((x + 3) % 4) * 4 + z),
            "z": (dp, x * 4 + (z + 3) % 4),
            "y": (((y + 3) % 4) * 2 + c, enc),
        }
        self.pos = {"x": x, "y": y, "z": z}
        self.partner = (y * 2 + (1 - c), enc)
        self.near = list(self.right.values()) + list(self.left.values()) + [self.partner]

    def column(self):
        steps = [(0, 1), (1, 0), (3, 0), (1, 1), (3, 1), (2, 0), (2, 1)]
        return [((self.y + dy) % 4, 1 - self.c if dc else self.c) for dy, dc in steps]

    def greet(self, others):
        sem = pltpu.get_barrier_semaphore()
        for other in others:
            pl.semaphore_signal(sem, inc=1, device_id=other, device_id_type=MESH)

    def meet(self, others):
        pl.semaphore_wait(pltpu.get_barrier_semaphore(), len(others))


class Copies:
    def __init__(self, send_sems, recv_sems):
        self.send_sems, self.recv_sems, self.used, self.started = send_sems, recv_sems, 0, []

    def start(self, src, dst, device):
        k = self.used
        self.used += 1
        copy = pltpu.make_async_remote_copy(
            src_ref=src,
            dst_ref=dst,
            send_sem=self.send_sems.at[k],
            recv_sem=self.recv_sems.at[k],
            device_id=device,
            device_id_type=MESH,
        )
        copy.start()
        self.started.append(copy)
        return copy

    def flush(self, some):
        for copy in some:
            copy.wait_send()
        gone = [id(copy) for copy in some]
        self.started = [copy for copy in self.started if id(copy) not in gone]

    def finish(self):
        self.flush(list(self.started))


class RingSum:
    def __init__(self, copies, place, axis, part, r1, r2):
        self.copies, self.part, self.r1, self.r2 = copies, part, r1, r2
        self.right, self.left = place.right[axis], place.left[axis]
        pos = place.pos[axis]
        self.pos, self.rt, self.lf, self.opp = pos, (pos + 1) % 4, (pos + 3) % 4, (pos + 2) % 4

    def send_opposite(self):
        self.a = self.copies.start(self.part(self.opp, 0), self.r1.at[0], self.right)
        self.b = self.copies.start(self.part(self.opp, 1), self.r1.at[1], self.left)

    def send_right(self):
        self.d = self.copies.start(self.part(self.rt, 1), self.r2.at[0, 1], self.right)

    def send_left(self):
        self.e = self.copies.start(self.part(self.lf, 0), self.r2.at[1, 0], self.left)

    def first(self):
        self.send_opposite()
        self.send_right()
        self.send_left()

    def second(self):
        self.a.wait_recv()
        mine = self.part(self.rt, 0)
        mine[...] = (mine[...].astype(F32) + self.r1[0].astype(F32)).astype(BF16)
        self.f = self.copies.start(mine, self.r2.at[0, 0], self.right)
        self.b.wait_recv()
        mine = self.part(self.lf, 1)
        mine[...] = (mine[...].astype(F32) + self.r1[1].astype(F32)).astype(BF16)
        self.g = self.copies.start(mine, self.r2.at[1, 1], self.left)

    def flush(self):
        self.copies.flush([self.a, self.b, self.d, self.e, self.f, self.g])

    def total(self):
        for copy in (self.d, self.e, self.f, self.g):
            copy.wait_recv()
        return [
            self.part(self.pos, h)[...].astype(F32)
            + self.r2[0, h].astype(F32)
            + self.r2[1, h].astype(F32)
            for h in (0, 1)
        ]


class RingGather:
    def __init__(self, copies, place, axis, block):
        self.copies, self.block = copies, block
        self.right, self.left = place.right[axis], place.left[axis]
        pos = place.pos[axis]
        self.pos, self.rt, self.lf = pos, (pos + 1) % 4, (pos + 3) % 4

    def first(self):
        own = self.block(self.pos, None)
        self.a = self.copies.start(own, own, self.right)
        self.b = self.copies.start(own, own, self.left)

    def second(self):
        self.a.wait_recv()
        part = self.block(self.lf, 0)
        self.d = self.copies.start(part, part, self.right)
        self.b.wait_recv()
        part = self.block(self.rt, 1)
        self.e = self.copies.start(part, part, self.left)

    def done(self):
        self.d.wait_recv()
        self.e.wait_recv()

    def flush(self):
        self.copies.flush([self.a, self.b, self.d, self.e])


HALVES = ((0, 128), (128, 256))


class PlaneSum:
    def __init__(self, copies, place, terms, sums, r1a, r2a, r1b, r2b):
        x, z = place.pos["x"], place.pos["z"]
        self.sums, self.place = sums, place

        def upper(b, h):
            return terms.at[b, 2 * h : 2 * h + 2, 0:128]

        def lower(b, h):
            return terms.at[2 * h : 2 * h + 2, b, 128:256]

        self.one = (
            RingSum(copies, place, "x", upper, r1a.at[0], r2a.at[0]),
            RingSum(copies, place, "z", lower, r1a.at[1], r2a.at[1]),
        )

        def upper_two(b, h):
            return sums.at[0, b, 64 * h : 64 * h + 64]

        def lower_two(b, h):
            return sums.at[1, b, 64 * h : 64 * h + 64]

        self.two = (
            RingSum(copies, place, "z", upper_two, r1b.at[0], r2b.at[0]),
            RingSum(copies, place, "x", lower_two, r1b.at[1], r2b.at[1]),
        )

    def opposite(self):
        for ring in self.one:
            ring.send_opposite()

    def sides(self):
        for ring in self.one:
            ring.send_right()
            ring.send_left()

    def step2(self):
        for ring in self.one:
            ring.second()

    def step3(self):
        for k in (0, 1):
            low, high = self.one[k].total()
            self.sums[k, 0:2] = low.astype(BF16)
            self.sums[k, 2:4] = high.astype(BF16)
            self.two[k].first()

    def step4(self):
        for ring in self.one:
            ring.flush()
        for ring in self.two:
            ring.second()

    def finish(self, store):
        for k in (0, 1):
            low, high = self.two[k].total()
            store(k * 128, low.astype(BF16))
            store(k * 128 + 64, high.astype(BF16))


class PlaneGather:
    def __init__(self, copies, place, buf):
        x, z = place.pos["x"], place.pos["z"]
        half = buf.shape[2] // 2
        quarter = half // 2

        def upper(b, h):
            if h is None:
                return buf.at[b, z, 0:half]
            return buf.at[b, z, quarter * h : quarter * h + quarter]

        def lower(b, h):
            if h is None:
                return buf.at[x, b, half : 2 * half]
            return buf.at[x, b, half + quarter * h : half + quarter * h + quarter]

        def upper_two(b, h):
            if h is None:
                return buf.at[:, b, 0:half]
            return buf.at[2 * h : 2 * h + 2, b, 0:half]

        def lower_two(b, h):
            if h is None:
                return buf.at[b, :, half : 2 * half]
            return buf.at[b, 2 * h : 2 * h + 2, half : 2 * half]

        self.one = (
            RingGather(copies, place, "x", upper),
            RingGather(copies, place, "z", lower),
        )
        self.two = (
            RingGather(copies, place, "z", upper_two),
            RingGather(copies, place, "x", lower_two),
        )

    def step1(self):
        for ring in self.one:
            ring.first()

    def step2(self):
        for ring in self.one:
            ring.second()

    def step3(self):
        for one, two in zip(self.one, self.two):
            one.done()
            two.first()

    def step4(self):
        for ring in self.two:
            ring.second()

    def done(self):
        for ring in self.two:
            ring.done()


def layer_kernel(
    nbrs,
    blocks,
    hidden,
    encodings,
    cotangent,
    wk_hbm,
    wv_hbm,
    wq_hbm,
    wo_hbm,
    layer_hbm,
    grad_hidden_hbm,
    grad_encodings_hbm,
    grad_wq_hbm,
    grad_wk_hbm,
    grad_wv_hbm,
    grad_wo_hbm,
    weights,
    out_weight,
    terms,
    sums,
    r1a,
    r2a,
    r1b,
    r2b,
    pair,
    cots,
    encs,
    hids,
    queries,
    grads,
    prob,
    scored,
    flipped,
    spread_v,
    spread_q,
    theirs,
    theirs_q,
    side_t,
    dense_in,
    dense_sum,
    dense_r,
    part_r1,
    part_r2,
    half_r1,
    half_r2,
    rows_out,
    grads_out,
    load_sems,
    send_sems,
    recv_sems,
):
    place = Place()
    x, y, z, c = place.x, place.y, place.z, place.c
    copies = Copies(send_sems, recv_sems)
    column = place.column()
    met = place.near + [(oy * 2 + oc, place.enc) for oy, oc in column[3:]]
    loads = [
        pltpu.make_async_copy(src, dst, load_sems.at[k])
        for k, (src, dst) in enumerate(
            [
                (wv_hbm, weights.at[1]),
                (wq_hbm, weights.at[2]),
                (wo_hbm, out_weight),
            ]
        )
    ]
    pieces = [
        pltpu.make_async_copy(
            wk_hbm.at[:, 1024 * b : 1024 * b + 1024],
            weights.at[0, :, 1024 * b : 1024 * b + 1024],
            load_sems.at[10 + b],
        )
        for b in range(4)
    ]
    for piece in pieces:
        piece.start()
    loads[0].start()
    place.greet(met)
    results = [
        pltpu.make_async_copy(src, dst, load_sems.at[3 + k])
        for k, (src, dst) in enumerate(
            [
                (rows_out.at[0], layer_hbm),
                (rows_out.at[1], grad_hidden_hbm),
                (rows_out.at[2], grad_encodings_hbm),
                (grads_out.at[0], grad_wq_hbm),
                (grads_out.at[1], grad_wk_hbm),
                (grads_out.at[2], grad_wv_hbm),
                (grads_out.at[3], grad_wo_hbm),
            ]
        )
    ]

    left = (encodings, encodings, hidden)
    keys, values, query, grad = [
        PlaneSum(
            copies, place, terms.at[k], sums.at[k], r1a.at[k], r2a.at[k], r1b.at[k], r2b.at[k]
        )
        for k in range(4)
    ]

    def first_terms():
        for b in range(4):
            pieces[b].wait()
            product = mm(encodings[...], weights[0, :, 1024 * b : 1024 * b + 1024]).astype(BF16)
            for i in range(4):
                terms[0, b, i] = product[:, i * 256 : i * 256 + 256]
        loads[1].start()
        loads[2].start()

    def make_terms(k):
        loads[k - 1].wait()
        rows = left[k][...]

        def body(b, carry):
            product = mm(rows, weights[k, :, columns(b)]).astype(BF16)
            for i in range(4):
                terms[k, b, i] = product[:, i * 256 : i * 256 + 256]
            return carry

        lax.fori_loop(0, 4, body, 0)

    def make_grad_terms():
        loads[2].wait()
        rows = cotangent[...]

        def body(b, carry):
            for i in range(4):
                span = pl.ds(pl.multiple_of(b * 1024 + i * 256, 256), 256)
                product = lax.dot_general(rows, out_weight[span, :], NT, preferred_element_type=F32)
                terms[3, b, i] = product.astype(BF16)
            return carry

        lax.fori_loop(0, 4, body, 0)

    def columns(b):
        return pl.ds(pl.multiple_of(b * 1024, 1024), 1024)

    def row_block(ref):
        def block(b, h):
            if h is None:
                return ref.at[b, c]
            return ref.at[b, c, 128 * h : 128 * h + 128]

        return block

    def pair_block(k):
        def block(b, h):
            if h is None:
                return pair.at[k, b, c]
            return pair.at[k, b, c, h]

        return block

    gather_encs = RingGather(copies, place, "y", row_block(encs))
    gather_hids = RingGather(copies, place, "y", row_block(hids))
    gather_keys, gather_values = [
        RingGather(copies, place, "y", pair_block(k)) for k in (0, 1)
    ]

    def swap(gather, mine):
        gather.done()
        return copies.start(mine, mine, place.partner)

    def store_pair(k):
        def store(row, value):
            at = row % 128
            pair[k, y, c, row // 128, at : at + 64] = value

        return store

    def store_to(ref):
        def store(row, value):
            ref[row : row + 64] = value

        return store

    scale = HD ** (-0.5)
    cases = [(t, h) for t in range(4) for h in range(2)]

    def rows_of(ref, t, h):
        return ref[t * 64 : t * 64 + 64, h * 128 : h * 128 + 128]

    def picked(which, t, h):
        return jnp.concatenate(
            [
                pair[which, n // 4, (n // 2) % 2, n % 2, :, h * 128 : h * 128 + 128]
                for n in (nbrs[0, t], nbrs[1, t])
            ],
            axis=0,
        )

    def attend():
        slot = lax.broadcasted_iota(jnp.int32, (64, 256), 1)
        for i, (t, h) in enumerate(cases):
            limit0 = BLK * blocks[nbrs[0, t]]
            limit1 = BLK * blocks[nbrs[1, t]]
            valid = slot < jnp.where(slot < 128, limit0, limit1 + 128)
            scores = (
                lax.dot_general(
                    rows_of(queries, t, h), picked(0, t, h), NT, preferred_element_type=F32
                )
                * scale
            )
            scores = jnp.where(valid, scores, -1e30)
            top = jnp.max(scores, axis=1, keepdims=True)
            exps = jnp.where(valid, jnp.exp(scores - top), 0.0)
            total = jnp.sum(exps, axis=1, keepdims=True)
            output = mm(exps.astype(BF16), picked(1, t, h)) / total
            terms[0, x, z, t * 64 : t * 64 + 64, h * 128 : h * 128 + 128] = output.astype(BF16)
            prob[h, t * 64 : t * 64 + 64] = exps / total

    def attend_back():
        for t, h in cases:
            weight = prob[h, t * 64 : t * 64 + 64]
            grad_prob = lax.dot_general(
                rows_of(grads, t, h), picked(1, t, h), NT, preferred_element_type=F32
            )
            inner = jnp.sum(weight * grad_prob, axis=1, keepdims=True)
            found = weight * (grad_prob - inner) * scale
            scored[h, t * 64 : t * 64 + 64] = found
            term = mm(found.astype(BF16), picked(0, t, h))
            terms[1, x, z, t * 64 : t * 64 + 64, h * 128 : h * 128 + 128] = term.astype(BF16)

    def flip(source):
        for h in range(2):
            flipped[h] = source[h].T

    def neighbour_grads(which, rows):
        lane = lax.broadcasted_iota(jnp.int32, (128, 256), 1)
        names = []
        for j in range(2):
            name = jnp.where(lane < 64, nbrs[j, 0], nbrs[j, 1])
            name = jnp.where(lane < 128, name, nbrs[j, 2])
            names.append(jnp.where(lane < 192, name, nbrs[j, 3]))

        def body(i, carry):
            for h in range(2):
                first, second = flipped[h, 0:128], flipped[h, 128:256]
                chosen = jnp.concatenate(
                    [
                        jnp.where(
                            names[0] == n,
                            first,
                            jnp.where(names[1] == n, second, jnp.zeros_like(first)),
                        )
                        for n in (2 * i, 2 * i + 1)
                    ],
                    axis=0,
                ).astype(BF16)
                term = mm(chosen, rows[:, h * 128 : h * 128 + 128]).astype(BF16)
                for j in range(2):
                    sums[
                        2 * which + i // 4, (i // 2) % 2, 2 * (i % 2) + j, :, h * 128 : h * 128 + 128
                    ] = term[j * 128 : j * 128 + 128]
            return carry

        lax.fori_loop(0, 8, body, 0)

    def swap_dense(k):
        return copies.start(
            sums.at[2 * k : 2 * k + 2, :, pl.ds(2 * (1 - c), 2)], dense_in.at[k], place.partner
        )

    def send_dense(k, swapped):
        swapped.wait_recv()
        for b in range(4):
            mine = sums[2 * k + b // 2, b % 2, pl.ds(2 * c, 2)]
            theirs_too = dense_in[k, b // 2, b % 2]
            dense_sum[b, k] = (mine.astype(F32) + theirs_too.astype(F32)).astype(BF16)
        return [
            copies.start(
                dense_sum.at[(y + step) % 4, k],
                dense_r.at[i, k],
                (((y + step) % 4) * 2 + c, place.enc),
            )
            for i, step in enumerate((1, 3, 2))
        ]

    def sum_dense(k, moves):
        for move in moves:
            move.wait_recv()
        total = dense_sum[y, k].astype(F32)
        for i in range(3):
            total = total + dense_r[i, k].astype(F32)
        terms[2 + k, x, z] = total.astype(BF16).reshape(256, 256)

    net_h, net_q, net_k, net_v = [PlaneGather(copies, place, terms.at[k]) for k in range(4)]
    net_sv, net_sq = [PlaneGather(copies, place, ref) for ref in (spread_v, spread_q)]

    def swap_half(k):
        return copies.start(terms.at[2 * k, :, pl.ds(2 * (1 - c), 2)], theirs.at[k], place.partner)

    class WeightGrad:
        def __init__(self, k):
            def part(b, h):
                return r2a.at[2 * k + b // 2, b % 2, h]

            self.k = k
            self.ring = RingSum(copies, place, "y", part, part_r1.at[k], part_r2.at[k])

        def block(self, b):
            k = self.k
            own = jnp.concatenate([terms[2 * k, b, 2 * c + i] for i in (0, 1)], axis=1)
            other = jnp.concatenate([theirs[k, b, i] for i in (0, 1)], axis=1)
            both = jnp.concatenate([own, other], axis=0)
            product = mm(side_t[2 * k], both).astype(BF16)
            for h in (0, 1):
                for i in (0, 1):
                    quarter = product[256 * h : 256 * h + 256, 256 * i : 256 * i + 256]
                    r2a[2 * k + b // 2, b % 2, h, i] = quarter.reshape(2, 128, 256)

        def one(self):
            self.block(self.ring.opp)
            self.ring.send_opposite()

        def two(self):
            self.block(self.ring.rt)
            self.ring.send_right()

        def three(self):
            self.block(self.ring.lf)
            self.ring.send_left()

        def four(self):
            self.block(self.ring.pos)

        def store(self):
            for h, found in enumerate(self.ring.total()):
                for i in (0, 1):
                    square = found[i].reshape(256, 256)
                    if self.k == 0:
                        grads_out[3, 256 * i : 256 * i + 256, 256 * h : 256 * h + 256] = square.T
                    else:
                        grads_out[1, 256 * h : 256 * h + 256, 256 * i : 256 * i + 256] = square
            results[6 if self.k == 0 else 4].start()

    class QueryGrad(WeightGrad):
        def __init__(self):
            def part(b, h):
                return pair.at[0, b, h]

            self.ring = RingSum(copies, place, "y", part, half_r1, half_r2)

        def block(self, b):
            both = jnp.concatenate([terms[1, b, 2 * c], theirs_q[b]], axis=0)
            product = mm(side_t[1], both).astype(BF16)
            pair[0, b] = product.reshape(2, 2, 128, 256)

        def store(self):
            for h, found in enumerate(self.ring.total()):
                grads_out[0, 256 * h : 256 * h + 256, 0:256] = found.reshape(256, 256)

    def wide(k, b):
        return jnp.concatenate([terms[k, b, i] for i in range(4)], axis=1)

    def accumulate(k, make, add=False, last=True):
        def body(b, carry):
            rows_out[k] += make(b)
            return carry

        if not add:
            rows_out[k] = make(0)
        lax.fori_loop(0 if add else 1, 4, body, 0)
        if last:
            results[k].start()

    def transposed(k, slot, b):
        return lax.dot_general(
            wide(k, b), weights[slot, :, columns(b)], NT, preferred_element_type=F32
        )

    def turn(source, store):
        def body(t, carry):
            rows = []
            for e in (2 * t, 2 * t + 1):
                span = pl.ds(pl.multiple_of(e * 16, 16), 16)
                rows += [source[d // 2, d % 2, span] for d in range(8)]
            store(t, jnp.concatenate(rows, axis=0).T)
            return carry

        lax.fori_loop(0, 8, body, 0)

    def store_encs(t, found):
        for i in range(4):
            r1a[t // 2, t % 2, i // 2, i % 2] = found[128 * i : 128 * i + 128]

    def store_hids(t, found):
        for i in range(4):
            sums[t // 2, t % 2, i] = found[128 * i : 128 * i + 128]

    def exchange_values():
        span = pl.ds(pl.multiple_of(place.enc * 16, 16), 16)
        spread_v[x, z, place.dp] = terms[3, y, pl.ds(2 * c, 2), span]
        return [
            copies.start(
                terms.at[3, oy, pl.ds(2 * oc, 2), span],
                spread_v.at[x, z, place.dp],
                (oy * 2 + oc, place.enc),
            )
            for oy, oc in column
        ]

    def exchange_queries():
        span = pl.ds(pl.multiple_of(place.enc * 16, 16), 16)
        spread_q[x, z, place.dp] = terms[1, y, 2 * c + 1, span]
        return [
            copies.start(
                terms.at[1, oy, 2 * oc + 1, span],
                spread_q.at[x, z, place.dp],
                (oy * 2 + oc, place.enc),
            )
            for oy, oc in column
        ]

    def whole_grad(turned, rows_of_part):
        total = None
        for b in range(4):
            sides = jnp.concatenate(
                [
                    jnp.concatenate([turned(b, j, i) for j in (0, 1)], axis=1)
                    for i in range(4)
                ],
                axis=0,
            )
            rows = jnp.concatenate([rows_of_part(b, k) for k in range(4)], axis=0)
            term = mm(sides, rows)
            total = term if total is None else total + term
        return total

    def value_rows(b, k):
        return jnp.concatenate([spread_v[b, k, :, i].reshape(128, 256) for i in (0, 1)], axis=1)

    def query_rows(b, k):
        return spread_q[b, k].reshape(128, 256)

    def turned_encs(b, j, i):
        return r1a[b, j, i // 2, i % 2]

    def turned_hids(b, j, i):
        return sums[b, j, i]

    cots[0] = cotangent[...]
    encs[y, c] = encodings[...]
    hids[y, c] = hidden[...]
    work_h, work_k, work_q = WeightGrad(0), WeightGrad(1), QueryGrad()
    first_terms()
    place.meet(met)
    keys.opposite()
    make_terms(1)
    values.opposite()
    keys.step2()
    keys.sides()
    gather_encs.first()
    make_terms(2)
    gather_hids.first()
    values.sides()
    values.step2()
    keys.step3()
    query.opposite()
    keys.step4()
    values.step3()
    query.sides()
    values.step4()
    query.step2()
    keys.finish(store_pair(0))
    gather_keys.first()
    make_grad_terms()
    values.finish(store_pair(1))
    gather_values.first()
    grad.opposite()
    gather_keys.second()
    query.step3()
    gather_values.second()
    grad.sides()
    query.step4()
    grad.step2()
    swap_keys = swap(gather_keys, pair.at[0, :, c])
    swap_values = swap(gather_values, pair.at[1, :, c])
    query.finish(store_to(queries))
    swap_keys.wait_recv()
    swap_values.wait_recv()
    attend()
    net_h.step1()
    gather_encs.second()
    grad.step3()
    net_h.step2()
    gather_hids.second()
    grad.step4()
    flip(prob)
    net_h.step3()
    swap_cots = copies.start(cots.at[0], cots.at[1], place.partner)
    grad.finish(store_to(grads))
    for total in (keys, values, query, grad):
        for ring in total.two:
            ring.flush()
    neighbour_grads(1, grads)
    swap_dense_v = swap_dense(1)
    attend_back()
    moves_dv = send_dense(1, swap_dense_v)
    net_q.step1()
    net_h.step4()
    swap_encs = swap(gather_encs, encs.at[:, c])
    flip(scored)
    neighbour_grads(0, queries)
    swap_dense_k = swap_dense(0)
    net_q.step2()
    sum_dense(1, moves_dv)
    net_v.step1()
    moves_dk = send_dense(0, swap_dense_k)
    net_h.done()
    net_q.step3()
    swap_h = swap_half(0)
    swap_cots.wait_recv()
    for k in (0, 1):
        side_t[0, :, k * 256 : k * 256 + 256] = cots[k].T
    net_v.step2()
    swap_h.wait_recv()
    work_h.one()
    swap_hids = swap(gather_hids, hids.at[:, c])
    work_h.two()
    work_h.three()
    sum_dense(0, moves_dk)
    net_k.step1()
    net_q.step4()
    gather_keys.flush()
    gather_values.flush()
    copies.flush([swap_keys, swap_values])
    net_k.step2()
    net_v.step3()
    net_q.done()
    work_h.ring.second()
    swap_hids.wait_recv()
    side_t[1, :, 0:256] = hids[y, c].T
    side_t[1, :, 256:512] = hids[y, 1 - c].T
    swap_q = copies.start(terms.at[1, :, 2 * (1 - c)], theirs_q, place.partner)
    net_k.step3()
    swap_encs.wait_recv()
    side_t[2, :, 0:256] = encs[y, c].T
    side_t[2, :, 256:512] = encs[y, 1 - c].T
    work_h.four()
    accumulate(1, lambda b: transposed(1, 2, b))
    net_v.step4()
    swap_q.wait_recv()
    work_q.one()
    copies.flush([swap_dense_v, swap_dense_k])
    turn(hids, store_hids)
    work_h.store()
    work_q.two()
    moves_q = exchange_queries()
    net_k.step4()
    work_q.three()
    net_v.done()
    moves_v = exchange_values()
    for move in moves_q:
        move.wait_recv()
    net_sq.step1()
    net_k.done()
    swap_k = swap_half(1)
    for move in moves_v:
        move.wait_recv()
    net_sv.step1()
    work_q.ring.second()
    accumulate(2, lambda b: transposed(3, 1, b), last=False)
    net_sq.step2()
    swap_k.wait_recv()
    work_k.one()
    net_sv.step2()
    net_sq.step3()
    work_k.two()
    work_k.three()
    work_q.four()
    net_sv.step3()
    net_sq.step4()
    work_k.ring.second()
    work_k.four()
    turn(encs, store_encs)
    accumulate(0, lambda b: mm(wide(0, b), out_weight[columns(b), :]))
    net_sv.step4()
    work_q.store()
    accumulate(2, lambda b: transposed(2, 0, b), add=True)
    net_sq.done()
    grads_out[0, :, 256:512] = whole_grad(turned_hids, query_rows)
    net_sv.done()
    results[3].start()
    grads_out[2] = whole_grad(turned_encs, value_rows)
    results[5].start()
    work_k.store()
    for k in range(7):
        results[k].wait()
    copies.finish()


def copy_kernel(*refs):
    sems = refs[-1]
    count = (len(refs) - 1) // 3
    loads, moves = [], []
    for k in range(count):
        held = refs[2 * count + k]
        loads.append(pltpu.make_async_copy(refs[k], held, sems.at[0, k]))
        moves.append(pltpu.make_async_copy(held, refs[count + k], sems.at[1, k]))
    for load in loads:
        load.start()
    for load, move in zip(loads, moves):
        load.wait()
        move.start()
    for move in moves:
        move.wait()


def vmem():
    return pl.BlockSpec(memory_space=pltpu.VMEM)


def hbm():
    return pl.BlockSpec(memory_space=pl.ANY)


def shape(*dims, dtype=BF16):
    return jax.ShapeDtypeStruct(dims, dtype)


def per_device(
    hidden,
    encodings,
    query_weight,
    key_weight,
    value_weight,
    out_weight,
    out_cotangent,
    stretch_nbrs,
    nbr_blocks,
):
    flat_enc = encodings.reshape(256, 512)
    dma = pltpu.SemaphoreType.DMA
    limit = 62 * 1024 * 1024
    results = [shape(256, 512, dtype=F32)] * 3 + [shape(512, 512, dtype=F32)] * 4
    outs = pl.pallas_call(
        layer_kernel,
        out_shape=results,
        in_specs=[pl.BlockSpec(memory_space=pltpu.SMEM)] * 2 + [vmem()] * 3 + [hbm()] * 4,
        out_specs=[hbm()] * 7,
        scratch_shapes=[
            pltpu.VMEM((3, 512, 4096), BF16),
            pltpu.VMEM((4096, 512), BF16),
            pltpu.VMEM((4, 4, 4, 256, 256), BF16),
            pltpu.VMEM((4, 2, 4, 128, 256), BF16),
            pltpu.VMEM((4, 2, 2, 2, 128, 256), BF16),
            pltpu.VMEM((4, 2, 2, 2, 2, 128, 256), BF16),
            pltpu.VMEM((4, 2, 2, 64, 256), BF16),
            pltpu.VMEM((4, 2, 2, 2, 64, 256), BF16),
            pltpu.VMEM((2, 4, 2, 2, 128, 256), BF16),
            pltpu.VMEM((2, 256, 512), BF16),
            pltpu.VMEM((4, 2, 256, 512), BF16),
            pltpu.VMEM((4, 2, 256, 512), BF16),
            pltpu.VMEM((256, 256), BF16),
            pltpu.VMEM((256, 256), BF16),
            pltpu.VMEM((2, 256, 256), F32),
            pltpu.VMEM((2, 256, 256), F32),
            pltpu.VMEM((2, 256, 256), F32),
            pltpu.VMEM((4, 4, 8, 2, 16, 256), BF16),
            pltpu.VMEM((4, 4, 8, 16, 256), BF16),
            pltpu.VMEM((2, 4, 2, 256, 256), BF16),
            pltpu.VMEM((4, 256, 256), BF16),
            pltpu.VMEM((3, 512, 512), BF16),
            pltpu.VMEM((2, 2, 2, 2, 128, 256), BF16),
            pltpu.VMEM((4, 2, 2, 128, 256), BF16),
            pltpu.VMEM((3, 2, 2, 128, 256), BF16),
            pltpu.VMEM((2, 2, 2, 2, 128, 256), BF16),
            pltpu.VMEM((2, 2, 2, 2, 2, 128, 256), BF16),
            pltpu.VMEM((2, 2, 128, 256), BF16),
            pltpu.VMEM((2, 2, 2, 128, 256), BF16),
            pltpu.VMEM((3, 256, 512), F32),
            pltpu.VMEM((4, 512, 512), F32),
            dma((14,)),
            dma((256,)),
            dma((256,)),
        ],
        compiler_params=pltpu.CompilerParams(
            collective_id=0, has_side_effects=True, vmem_limit_bytes=limit
        ),
    )(
        stretch_nbrs.T,
        nbr_blocks,
        hidden,
        flat_enc,
        out_cotangent,
        key_weight,
        value_weight,
        query_weight,
        out_weight,
    )
    outs = pl.pallas_call(
        copy_kernel,
        out_shape=results,
        in_specs=[hbm()] * 7,
        out_specs=[hbm()] * 7,
        scratch_shapes=[pltpu.VMEM(r.shape, F32) for r in results] + [dma((2, 7))],
        compiler_params=pltpu.CompilerParams(vmem_limit_bytes=limit),
    )(*outs)
    layer_out, grad_hidden, grad_enc, grad_wq, grad_wk, grad_wv, grad_wo = outs
    return (
        layer_out,
        grad_hidden,
        grad_enc.reshape(encodings.shape),
        grad_wq,
        grad_wk,
        grad_wv,
        grad_wo,
    )


def solution(mesh):
    in_specs = (
        P("dp", "enc"),
        P("dp", None, "enc"),
        P("enc", None),
        P("enc", None),
        P("enc", None),
        P(None, "enc"),
        P("dp", "enc"),
        P("dp", None),
        P(),
    )
    out_specs = (
        P("dp", "enc"),
        P("dp", "enc"),
        P("dp", None, "enc"),
        P("enc", "dp"),
        P("enc", "dp"),
        P("enc", "dp"),
        P("dp", "enc"),
    )
    return jax.shard_map(
        per_device, mesh=mesh, in_specs=in_specs, out_specs=out_specs, check_vma=False
    )
```

```python
import functools

import jax
import jax.numpy as jnp
from jax import lax
from jax.experimental import pallas as pl
from jax.experimental.pallas import tpu as pltpu
from jax.sharding import PartitionSpec as P

HD = 128
BLK = 16
MESH = pl.DeviceIdType.MESH
F32 = jnp.float32
BF16 = jnp.bfloat16
NT = (((1,), (1,)), ((), ()))
TN = (((0,), (0,)), ((), ()))


def mm(a, b):
    return jnp.dot(a, b, preferred_element_type=F32)


class Place:
    def __init__(self):
        self.dp = lax.axis_index("dp")
        self.enc = lax.axis_index("enc")
        dp, enc = self.dp, self.enc
        self.y, self.c = dp // 2, dp % 2
        self.x, self.z = enc // 4, enc % 4
        x, y, z, c = self.x, self.y, self.z, self.c
        self.right = {
            "x": (dp, ((x + 1) % 4) * 4 + z),
            "z": (dp, x * 4 + (z + 1) % 4),
            "y": (((y + 1) % 4) * 2 + c, enc),
        }
        self.left = {
            "x": (dp, ((x + 3) % 4) * 4 + z),
            "z": (dp, x * 4 + (z + 3) % 4),
            "y": (((y + 3) % 4) * 2 + c, enc),
        }
        self.pos = {"x": x, "y": y, "z": z}
        self.partner = (y * 2 + (1 - c), enc)
        self.near = list(self.right.values()) + list(self.left.values()) + [self.partner]

    def column(self):
        steps = [(0, 1), (1, 0), (3, 0), (1, 1), (3, 1), (2, 0), (2, 1)]
        return [((self.y + dy) % 4, 1 - self.c if dc else self.c) for dy, dc in steps]

    def greet(self, others):
        sem = pltpu.get_barrier_semaphore()
        for other in others:
            pl.semaphore_signal(sem, inc=1, device_id=other, device_id_type=MESH)

    def meet(self, others):
        pl.semaphore_wait(pltpu.get_barrier_semaphore(), len(others))


class Copies:
    def __init__(self, send_sems, recv_sems):
        self.send_sems, self.recv_sems, self.used, self.started = send_sems, recv_sems, 0, []

    def start(self, src, dst, device):
        k = self.used
        self.used += 1
        copy = pltpu.make_async_remote_copy(
            src_ref=src,
            dst_ref=dst,
            send_sem=self.send_sems.at[k],
            recv_sem=self.recv_sems.at[k],
            device_id=device,
            device_id_type=MESH,
        )
        copy.start()
        self.started.append(copy)
        return copy

    def flush(self, some):
        for copy in some:
            copy.wait_send()
        gone = [id(copy) for copy in some]
        self.started = [copy for copy in self.started if id(copy) not in gone]

    def finish(self):
        self.flush(list(self.started))


class RingSum:
    def __init__(self, copies, place, axis, part, r1, r2):
        self.copies, self.part, self.r1, self.r2 = copies, part, r1, r2
        self.right, self.left = place.right[axis], place.left[axis]
        pos = place.pos[axis]
        self.pos, self.rt, self.lf, self.opp = pos, (pos + 1) % 4, (pos + 3) % 4, (pos + 2) % 4

    def send_opposite(self):
        self.a = self.copies.start(self.part(self.opp, 0), self.r1.at[0], self.right)
        self.b = self.copies.start(self.part(self.opp, 1), self.r1.at[1], self.left)

    def send_right(self):
        self.d = self.copies.start(self.part(self.rt, 1), self.r2.at[0, 1], self.right)

    def send_left(self):
        self.e = self.copies.start(self.part(self.lf, 0), self.r2.at[1, 0], self.left)

    def first(self):
        self.send_opposite()
        self.send_right()
        self.send_left()

    def second(self):
        self.a.wait_recv()
        mine = self.part(self.rt, 0)
        mine[...] = (mine[...].astype(F32) + self.r1[0].astype(F32)).astype(BF16)
        self.f = self.copies.start(mine, self.r2.at[0, 0], self.right)
        self.b.wait_recv()
        mine = self.part(self.lf, 1)
        mine[...] = (mine[...].astype(F32) + self.r1[1].astype(F32)).astype(BF16)
        self.g = self.copies.start(mine, self.r2.at[1, 1], self.left)

    def flush(self):
        self.copies.flush([self.a, self.b, self.d, self.e, self.f, self.g])

    def total(self):
        for copy in (self.d, self.e, self.f, self.g):
            copy.wait_recv()
        return [
            self.part(self.pos, h)[...].astype(F32)
            + self.r2[0, h].astype(F32)
            + self.r2[1, h].astype(F32)
            for h in (0, 1)
        ]


class RingGather:
    def __init__(self, copies, place, axis, block):
        self.copies, self.block = copies, block
        self.right, self.left = place.right[axis], place.left[axis]
        pos = place.pos[axis]
        self.pos, self.rt, self.lf = pos, (pos + 1) % 4, (pos + 3) % 4

    def first(self):
        own = self.block(self.pos, None)
        self.a = self.copies.start(own, own, self.right)
        self.b = self.copies.start(own, own, self.left)

    def second(self):
        self.a.wait_recv()
        part = self.block(self.lf, 0)
        self.d = self.copies.start(part, part, self.right)
        self.b.wait_recv()
        part = self.block(self.rt, 1)
        self.e = self.copies.start(part, part, self.left)

    def done(self):
        self.d.wait_recv()
        self.e.wait_recv()

    def flush(self):
        self.copies.flush([self.a, self.b, self.d, self.e])


HALVES = ((0, 128), (128, 256))


class PlaneSum:
    def __init__(self, copies, place, terms, sums, r1a, r2a, r1b, r2b):
        x, z = place.pos["x"], place.pos["z"]
        self.sums, self.place = sums, place

        def upper(b, h):
            return terms.at[b, 2 * h : 2 * h + 2, 0:128]

        def lower(b, h):
            return terms.at[2 * h : 2 * h + 2, b, 128:256]

        self.one = (
            RingSum(copies, place, "x", upper, r1a.at[0], r2a.at[0]),
            RingSum(copies, place, "z", lower, r1a.at[1], r2a.at[1]),
        )

        def upper_two(b, h):
            return sums.at[0, b, 64 * h : 64 * h + 64]

        def lower_two(b, h):
            return sums.at[1, b, 64 * h : 64 * h + 64]

        self.two = (
            RingSum(copies, place, "z", upper_two, r1b.at[0], r2b.at[0]),
            RingSum(copies, place, "x", lower_two, r1b.at[1], r2b.at[1]),
        )

    def opposite(self):
        for ring in self.one:
            ring.send_opposite()

    def sides(self):
        for ring in self.one:
            ring.send_right()
            ring.send_left()

    def step2(self):
        for ring in self.one:
            ring.second()

    def step3(self):
        for k in (0, 1):
            low, high = self.one[k].total()
            self.sums[k, 0:2] = low.astype(BF16)
            self.sums[k, 2:4] = high.astype(BF16)
            self.two[k].first()

    def step4(self):
        for ring in self.one:
            ring.flush()
        for ring in self.two:
            ring.second()

    def finish(self, store):
        for k in (0, 1):
            low, high = self.two[k].total()
            store(k * 128, low.astype(BF16))
            store(k * 128 + 64, high.astype(BF16))


class PlaneGather:
    def __init__(self, copies, place, buf):
        self.copies = copies
        half = buf.shape[2] // 2
        self.ways = [self.way(copies, place, buf, half, k) for k in (0, 1)]

    def way(self, copies, place, buf, half, k):
        axes = ("x", "z") if k == 0 else ("z", "x")
        near, far = [place.pos[axis] for axis in axes]
        quarter = half // 2
        start = k * half

        def cells(i, j, rows):
            return buf.at[i, j, rows] if k == 0 else buf.at[j, i, rows]

        def block(b, h):
            if h is None:
                return cells(b, far, slice(start, start + half))
            low = start + quarter * h
            return cells(b, far, slice(low, low + quarter))

        def pair_of(h, j):
            return cells(slice(2 * h, 2 * h + 2), j, slice(start, start + half))

        return {
            "ring": RingGather(copies, place, axes[0], block),
            "block": block,
            "pair": pair_of,
            "near": near,
            "far": far,
            "right": place.right[axes[1]],
            "left": place.left[axes[1]],
            "from_left": [],
            "from_right": [],
        }

    def send(self, way, step):
        cell = way["block"]((way["near"] + step) % 4, None)
        way["from_left"].append(self.copies.start(cell, cell, way["right"]))
        way["from_right"].append(self.copies.start(cell, cell, way["left"]))

    def step1(self):
        for way in self.ways:
            way["ring"].first()
        for way in self.ways:
            self.send(way, 0)

    def step2(self):
        for way in self.ways:
            way["ring"].second()
        for way in self.ways:
            self.send(way, 1)
            self.send(way, 3)

    def step3(self):
        for way in self.ways:
            way["ring"].done()
            self.send(way, 2)

    def step4(self):
        for way in self.ways:
            for copy in way["from_left"]:
                copy.wait_recv()
            part = way["pair"](0, (way["far"] + 3) % 4)
            way["d"] = self.copies.start(part, part, way["right"])
            for copy in way["from_right"]:
                copy.wait_recv()
            part = way["pair"](1, (way["far"] + 1) % 4)
            way["e"] = self.copies.start(part, part, way["left"])

    def done(self):
        for way in self.ways:
            way["d"].wait_recv()
            way["e"].wait_recv()


def layer_kernel(
    nbrs,
    blocks,
    hidden,
    encodings,
    cotangent,
    wk_hbm,
    wv_hbm,
    wq_hbm,
    wo_hbm,
    layer_hbm,
    grad_hidden_hbm,
    grad_encodings_hbm,
    grad_wq_hbm,
    grad_wk_hbm,
    grad_wv_hbm,
    grad_wo_hbm,
    weights,
    out_weight,
    terms,
    sums,
    r1a,
    r2a,
    r1b,
    r2b,
    pair,
    cots,
    encs,
    hids,
    queries,
    grads,
    prob,
    scored,
    flipped,
    spread_v,
    spread_q,
    theirs,
    theirs_q,
    side_t,
    dense_in,
    dense_sum,
    dense_r,
    part_r1,
    part_r2,
    half_r1,
    half_r2,
    rows_out,
    grads_out,
    load_sems,
    send_sems,
    recv_sems,
):
    place = Place()
    x, y, z, c = place.x, place.y, place.z, place.c
    copies = Copies(send_sems, recv_sems)
    column = place.column()
    met = place.near + [(oy * 2 + oc, place.enc) for oy, oc in column[3:]]
    loads = [
        pltpu.make_async_copy(src, dst, load_sems.at[k])
        for k, (src, dst) in enumerate(
            [
                (wv_hbm, weights.at[1]),
                (wq_hbm, weights.at[2]),
                (wo_hbm, out_weight),
            ]
        )
    ]
    pieces = [
        pltpu.make_async_copy(
            wk_hbm.at[:, 1024 * b : 1024 * b + 1024],
            weights.at[0, :, 1024 * b : 1024 * b + 1024],
            load_sems.at[10 + b],
        )
        for b in range(4)
    ]
    for piece in pieces:
        piece.start()
    loads[0].start()
    place.greet(met)
    results = [
        pltpu.make_async_copy(src, dst, load_sems.at[3 + k])
        for k, (src, dst) in enumerate(
            [
                (rows_out.at[0], layer_hbm),
                (rows_out.at[1], grad_hidden_hbm),
                (rows_out.at[2], grad_encodings_hbm),
                (grads_out.at[0], grad_wq_hbm),
                (grads_out.at[1], grad_wk_hbm),
                (grads_out.at[2], grad_wv_hbm),
                (grads_out.at[3], grad_wo_hbm),
            ]
        )
    ]

    left = (encodings, encodings, hidden)
    keys, values, query, grad = [
        PlaneSum(
            copies, place, terms.at[k], sums.at[k], r1a.at[k], r2a.at[k], r1b.at[k], r2b.at[k]
        )
        for k in range(4)
    ]

    def first_terms():
        for b in range(4):
            pieces[b].wait()
            product = mm(encodings[...], weights[0, :, 1024 * b : 1024 * b + 1024]).astype(BF16)
            for i in range(4):
                terms[0, b, i] = product[:, i * 256 : i * 256 + 256]
        loads[1].start()
        loads[2].start()

    def make_terms(k):
        loads[k - 1].wait()
        rows = left[k][...]

        def body(b, carry):
            product = mm(rows, weights[k, :, columns(b)]).astype(BF16)
            for i in range(4):
                terms[k, b, i] = product[:, i * 256 : i * 256 + 256]
            return carry

        lax.fori_loop(0, 4, body, 0)

    def make_grad_terms():
        loads[2].wait()
        rows = cotangent[...]

        def body(b, carry):
            for i in range(4):
                span = pl.ds(pl.multiple_of(b * 1024 + i * 256, 256), 256)
                product = lax.dot_general(rows, out_weight[span, :], NT, preferred_element_type=F32)
                terms[3, b, i] = product.astype(BF16)
            return carry

        lax.fori_loop(0, 4, body, 0)

    def columns(b):
        return pl.ds(pl.multiple_of(b * 1024, 1024), 1024)

    def row_block(ref):
        def block(b, h):
            if h is None:
                return ref.at[b, c]
            return ref.at[b, c, 128 * h : 128 * h + 128]

        return block

    def pair_block(k):
        def block(b, h):
            if h is None:
                return pair.at[k, b, c]
            return pair.at[k, b, c, h]

        return block

    gather_encs = RingGather(copies, place, "y", row_block(encs))
    gather_hids = RingGather(copies, place, "y", row_block(hids))
    gather_keys, gather_values = [
        RingGather(copies, place, "y", pair_block(k)) for k in (0, 1)
    ]

    def swap(gather, mine):
        gather.done()
        return copies.start(mine, mine, place.partner)

    def store_pair(k):
        def store(row, value):
            at = row % 128
            pair[k, y, c, row // 128, at : at + 64] = value

        return store

    def store_to(ref):
        def store(row, value):
            ref[row : row + 64] = value

        return store

    scale = HD ** (-0.5)
    cases = [(t, h) for t in range(4) for h in range(2)]

    def rows_of(ref, t, h):
        return ref[t * 64 : t * 64 + 64, h * 128 : h * 128 + 128]

    def picked(which, t, h):
        return jnp.concatenate(
            [
                pair[which, n // 4, (n // 2) % 2, n % 2, :, h * 128 : h * 128 + 128]
                for n in (nbrs[0, t], nbrs[1, t])
            ],
            axis=0,
        )

    def attend():
        slot = lax.broadcasted_iota(jnp.int32, (64, 256), 1)
        for i, (t, h) in enumerate(cases):
            limit0 = BLK * blocks[nbrs[0, t]]
            limit1 = BLK * blocks[nbrs[1, t]]
            valid = slot < jnp.where(slot < 128, limit0, limit1 + 128)
            scores = (
                lax.dot_general(
                    rows_of(queries, t, h), picked(0, t, h), NT, preferred_element_type=F32
                )
                * scale
            )
            scores = jnp.where(valid, scores, -1e30)
            top = jnp.max(scores, axis=1, keepdims=True)
            exps = jnp.where(valid, jnp.exp(scores - top), 0.0)
            total = jnp.sum(exps, axis=1, keepdims=True)
            output = mm(exps.astype(BF16), picked(1, t, h)) / total
            terms[0, x, z, t * 64 : t * 64 + 64, h * 128 : h * 128 + 128] = output.astype(BF16)
            prob[h, t * 64 : t * 64 + 64] = exps / total

    def attend_back():
        for t, h in cases:
            weight = prob[h, t * 64 : t * 64 + 64]
            grad_prob = lax.dot_general(
                rows_of(grads, t, h), picked(1, t, h), NT, preferred_element_type=F32
            )
            inner = jnp.sum(weight * grad_prob, axis=1, keepdims=True)
            found = weight * (grad_prob - inner) * scale
            scored[h, t * 64 : t * 64 + 64] = found
            term = mm(found.astype(BF16), picked(0, t, h))
            terms[1, x, z, t * 64 : t * 64 + 64, h * 128 : h * 128 + 128] = term.astype(BF16)

    def flip(source):
        for h in range(2):
            flipped[h] = source[h].T

    def neighbour_grads(which, rows):
        lane = lax.broadcasted_iota(jnp.int32, (128, 256), 1)
        names = []
        for j in range(2):
            name = jnp.where(lane < 64, nbrs[j, 0], nbrs[j, 1])
            name = jnp.where(lane < 128, name, nbrs[j, 2])
            names.append(jnp.where(lane < 192, name, nbrs[j, 3]))

        def body(i, carry):
            for h in range(2):
                first, second = flipped[h, 0:128], flipped[h, 128:256]
                chosen = jnp.concatenate(
                    [
                        jnp.where(
                            names[0] == n,
                            first,
                            jnp.where(names[1] == n, second, jnp.zeros_like(first)),
                        )
                        for n in (2 * i, 2 * i + 1)
                    ],
                    axis=0,
                ).astype(BF16)
                term = mm(chosen, rows[:, h * 128 : h * 128 + 128]).astype(BF16)
                for j in range(2):
                    sums[
                        2 * which + i // 4, (i // 2) % 2, 2 * (i % 2) + j, :, h * 128 : h * 128 + 128
                    ] = term[j * 128 : j * 128 + 128]
            return carry

        lax.fori_loop(0, 8, body, 0)

    def swap_dense(k):
        return copies.start(
            sums.at[2 * k : 2 * k + 2, :, pl.ds(2 * (1 - c), 2)], dense_in.at[k], place.partner
        )

    def send_dense(k, swapped):
        swapped.wait_recv()
        for b in range(4):
            mine = sums[2 * k + b // 2, b % 2, pl.ds(2 * c, 2)]
            theirs_too = dense_in[k, b // 2, b % 2]
            dense_sum[b, k] = (mine.astype(F32) + theirs_too.astype(F32)).astype(BF16)
        return [
            copies.start(
                dense_sum.at[(y + step) % 4, k],
                dense_r.at[i, k],
                (((y + step) % 4) * 2 + c, place.enc),
            )
            for i, step in enumerate((1, 3, 2))
        ]

    def sum_dense(k, moves):
        for move in moves:
            move.wait_recv()
        total = dense_sum[y, k].astype(F32)
        for i in range(3):
            total = total + dense_r[i, k].astype(F32)
        terms[2 + k, x, z] = total.astype(BF16).reshape(256, 256)

    net_h, net_q, net_k, net_v = [PlaneGather(copies, place, terms.at[k]) for k in range(4)]
    net_sv, net_sq = [PlaneGather(copies, place, ref) for ref in (spread_v, spread_q)]

    def swap_half(k):
        return copies.start(terms.at[2 * k, :, pl.ds(2 * (1 - c), 2)], theirs.at[k], place.partner)

    class WeightGrad:
        def __init__(self, k):
            def part(b, h):
                return r2a.at[2 * k + b // 2, b % 2, h]

            self.k = k
            self.ring = RingSum(copies, place, "y", part, part_r1.at[k], part_r2.at[k])

        def block(self, b):
            k = self.k
            own = jnp.concatenate([terms[2 * k, b, 2 * c + i] for i in (0, 1)], axis=1)
            other = jnp.concatenate([theirs[k, b, i] for i in (0, 1)], axis=1)
            both = jnp.concatenate([own, other], axis=0)
            product = mm(side_t[2 * k], both).astype(BF16)
            for h in (0, 1):
                for i in (0, 1):
                    quarter = product[256 * h : 256 * h + 256, 256 * i : 256 * i + 256]
                    r2a[2 * k + b // 2, b % 2, h, i] = quarter.reshape(2, 128, 256)

        def one(self):
            self.block(self.ring.opp)
            self.ring.send_opposite()

        def two(self):
            self.block(self.ring.rt)
            self.ring.send_right()

        def three(self):
            self.block(self.ring.lf)
            self.ring.send_left()

        def four(self):
            self.block(self.ring.pos)

        def store(self):
            for h, found in enumerate(self.ring.total()):
                for i in (0, 1):
                    square = found[i].reshape(256, 256)
                    if self.k == 0:
                        grads_out[3, 256 * i : 256 * i + 256, 256 * h : 256 * h + 256] = square.T
                    else:
                        grads_out[1, 256 * h : 256 * h + 256, 256 * i : 256 * i + 256] = square
            results[6 if self.k == 0 else 4].start()

    class QueryGrad(WeightGrad):
        def __init__(self):
            def part(b, h):
                return pair.at[0, b, h]

            self.ring = RingSum(copies, place, "y", part, half_r1, half_r2)

        def block(self, b):
            both = jnp.concatenate([terms[1, b, 2 * c], theirs_q[b]], axis=0)
            product = mm(side_t[1], both).astype(BF16)
            pair[0, b] = product.reshape(2, 2, 128, 256)

        def store(self):
            for h, found in enumerate(self.ring.total()):
                grads_out[0, 256 * h : 256 * h + 256, 0:256] = found.reshape(256, 256)

    def wide(k, b):
        return jnp.concatenate([terms[k, b, i] for i in range(4)], axis=1)

    def accumulate(k, make, add=False, last=True):
        def body(b, carry):
            rows_out[k] += make(b)
            return carry

        if not add:
            rows_out[k] = make(0)
        lax.fori_loop(0 if add else 1, 4, body, 0)
        if last:
            results[k].start()

    def transposed(k, slot, b):
        return lax.dot_general(
            wide(k, b), weights[slot, :, columns(b)], NT, preferred_element_type=F32
        )

    def turn(source, store):
        def body(t, carry):
            rows = []
            for e in (2 * t, 2 * t + 1):
                span = pl.ds(pl.multiple_of(e * 16, 16), 16)
                rows += [source[d // 2, d % 2, span] for d in range(8)]
            store(t, jnp.concatenate(rows, axis=0).T)
            return carry

        lax.fori_loop(0, 8, body, 0)

    def store_encs(t, found):
        for i in range(4):
            r1a[t // 2, t % 2, i // 2, i % 2] = found[128 * i : 128 * i + 128]

    def store_hids(t, found):
        for i in range(4):
            sums[t // 2, t % 2, i] = found[128 * i : 128 * i + 128]

    def exchange_values():
        span = pl.ds(pl.multiple_of(place.enc * 16, 16), 16)
        spread_v[x, z, place.dp] = terms[3, y, pl.ds(2 * c, 2), span]
        return [
            copies.start(
                terms.at[3, oy, pl.ds(2 * oc, 2), span],
                spread_v.at[x, z, place.dp],
                (oy * 2 + oc, place.enc),
            )
            for oy, oc in column
        ]

    def exchange_queries():
        span = pl.ds(pl.multiple_of(place.enc * 16, 16), 16)
        spread_q[x, z, place.dp] = terms[1, y, 2 * c + 1, span]
        return [
            copies.start(
                terms.at[1, oy, 2 * oc + 1, span],
                spread_q.at[x, z, place.dp],
                (oy * 2 + oc, place.enc),
            )
            for oy, oc in column
        ]

    def whole_grad(turned, rows_of_part):
        total = None
        for b in range(4):
            sides = jnp.concatenate(
                [
                    jnp.concatenate([turned(b, j, i) for j in (0, 1)], axis=1)
                    for i in range(4)
                ],
                axis=0,
            )
            rows = jnp.concatenate([rows_of_part(b, k) for k in range(4)], axis=0)
            term = mm(sides, rows)
            total = term if total is None else total + term
        return total

    def value_rows(b, k):
        return jnp.concatenate([spread_v[b, k, :, i].reshape(128, 256) for i in (0, 1)], axis=1)

    def query_rows(b, k):
        return spread_q[b, k].reshape(128, 256)

    def turned_encs(b, j, i):
        return r1a[b, j, i // 2, i % 2]

    def turned_hids(b, j, i):
        return sums[b, j, i]

    cots[0] = cotangent[...]
    encs[y, c] = encodings[...]
    hids[y, c] = hidden[...]
    work_h, work_k, work_q = WeightGrad(0), WeightGrad(1), QueryGrad()
    first_terms()
    place.meet(met)
    keys.opposite()
    make_terms(1)
    values.opposite()
    keys.sides()
    gather_hids.first()
    keys.step2()
    values.sides()
    make_terms(2)
    gather_hids.second()
    values.step2()
    make_grad_terms()
    gather_encs.first()
    keys.step3()
    query.opposite()
    keys.step4()
    values.step3()
    query.sides()
    keys.finish(store_pair(0))
    gather_encs.second()
    values.step4()
    gather_keys.first()
    query.step2()
    values.finish(store_pair(1))
    gather_values.first()
    grad.opposite()
    grad.sides()
    gather_keys.second()
    query.step3()
    gather_values.second()
    grad.step2()
    query.step4()
    swap_values = swap(gather_values, pair.at[1, :, c])
    swap_keys = swap(gather_keys, pair.at[0, :, c])
    grad.step3()
    query.finish(store_to(queries))
    swap_keys.wait_recv()
    swap_values.wait_recv()
    attend()
    net_h.step1()
    swap_hids = swap(gather_hids, hids.at[:, c])
    grad.step4()
    net_h.step2()
    flip(prob)
    grad.finish(store_to(grads))
    for total in (keys, values, query, grad):
        for ring in total.two:
            ring.flush()
    attend_back()
    net_h.step3()
    neighbour_grads(1, grads)
    swap_dense_v = swap_dense(1)
    net_q.step1()
    flip(scored)
    neighbour_grads(0, queries)
    swap_dense_k = swap_dense(0)
    net_h.step4()
    moves_dv = send_dense(1, swap_dense_v)
    net_q.step2()
    swap_cots = copies.start(cots.at[0], cots.at[1], place.partner)
    moves_dk = send_dense(0, swap_dense_k)
    net_h.done()
    swap_h = swap_half(0)
    net_q.step3()
    swap_cots.wait_recv()
    for k in (0, 1):
        side_t[0, :, k * 256 : k * 256 + 256] = cots[k].T
    sum_dense(1, moves_dv)
    swap_hids.wait_recv()
    side_t[1, :, 0:256] = hids[y, c].T
    side_t[1, :, 256:512] = hids[y, 1 - c].T
    net_v.step1()
    swap_h.wait_recv()
    work_h.one()
    net_q.step4()
    work_h.two()
    gather_keys.flush()
    gather_values.flush()
    copies.flush([swap_keys, swap_values])
    sum_dense(0, moves_dk)
    net_k.step1()
    work_h.three()
    net_q.done()
    net_v.step2()
    swap_encs = swap(gather_encs, encs.at[:, c])
    work_h.ring.second()
    net_k.step2()
    moves_q = exchange_queries()
    swap_q = copies.start(terms.at[1, :, 2 * (1 - c)], theirs_q, place.partner)
    net_k.step3()
    net_v.step3()
    accumulate(0, lambda b: mm(wide(0, b), out_weight[columns(b), :]))
    swap_q.wait_recv()
    work_q.one()
    work_q.two()
    work_q.three()
    net_k.step4()
    net_v.step4()
    work_h.four()
    accumulate(1, lambda b: transposed(1, 2, b))
    swap_encs.wait_recv()
    side_t[2, :, 0:256] = encs[y, c].T
    side_t[2, :, 256:512] = encs[y, 1 - c].T
    work_q.ring.second()
    net_k.done()
    swap_k = swap_half(1)
    for move in moves_q:
        move.wait_recv()
    net_sq.step1()
    net_v.done()
    moves_v = exchange_values()
    net_sq.step2()
    swap_k.wait_recv()
    work_k.one()
    work_q.four()
    for move in moves_v:
        move.wait_recv()
    net_sv.step1()
    work_k.two()
    net_sq.step3()
    work_k.three()
    copies.flush([swap_dense_v, swap_dense_k])
    turn(hids, store_hids)
    net_sv.step2()
    accumulate(2, lambda b: transposed(3, 1, b), last=False)
    net_sv.step3()
    work_k.ring.second()
    work_h.store()
    work_k.four()
    net_sq.step4()
    work_q.store()
    turn(encs, store_encs)
    net_sv.step4()
    net_sq.done()
    accumulate(2, lambda b: transposed(2, 0, b), add=True)
    grads_out[0, :, 256:512] = whole_grad(turned_hids, query_rows)
    net_sv.done()
    results[3].start()
    grads_out[2] = whole_grad(turned_encs, value_rows)
    results[5].start()
    work_k.store()
    for k in range(7):
        results[k].wait()
    copies.finish()


def copy_kernel(*refs):
    sems = refs[-1]
    count = (len(refs) - 1) // 3
    loads, moves = [], []
    for k in range(count):
        held = refs[2 * count + k]
        loads.append(pltpu.make_async_copy(refs[k], held, sems.at[0, k]))
        moves.append(pltpu.make_async_copy(held, refs[count + k], sems.at[1, k]))
    for load in loads:
        load.start()
    for load, move in zip(loads, moves):
        load.wait()
        move.start()
    for move in moves:
        move.wait()


def vmem():
    return pl.BlockSpec(memory_space=pltpu.VMEM)


def hbm():
    return pl.BlockSpec(memory_space=pl.ANY)


def shape(*dims, dtype=BF16):
    return jax.ShapeDtypeStruct(dims, dtype)


def per_device(
    hidden,
    encodings,
    query_weight,
    key_weight,
    value_weight,
    out_weight,
    out_cotangent,
    stretch_nbrs,
    nbr_blocks,
):
    flat_enc = encodings.reshape(256, 512)
    dma = pltpu.SemaphoreType.DMA
    limit = 62 * 1024 * 1024
    results = [shape(256, 512, dtype=F32)] * 3 + [shape(512, 512, dtype=F32)] * 4
    outs = pl.pallas_call(
        layer_kernel,
        out_shape=results,
        in_specs=[pl.BlockSpec(memory_space=pltpu.SMEM)] * 2 + [vmem()] * 3 + [hbm()] * 4,
        out_specs=[hbm()] * 7,
        scratch_shapes=[
            pltpu.VMEM((3, 512, 4096), BF16),
            pltpu.VMEM((4096, 512), BF16),
            pltpu.VMEM((4, 4, 4, 256, 256), BF16),
            pltpu.VMEM((4, 2, 4, 128, 256), BF16),
            pltpu.VMEM((4, 2, 2, 2, 128, 256), BF16),
            pltpu.VMEM((4, 2, 2, 2, 2, 128, 256), BF16),
            pltpu.VMEM((4, 2, 2, 64, 256), BF16),
            pltpu.VMEM((4, 2, 2, 2, 64, 256), BF16),
            pltpu.VMEM((2, 4, 2, 2, 128, 256), BF16),
            pltpu.VMEM((2, 256, 512), BF16),
            pltpu.VMEM((4, 2, 256, 512), BF16),
            pltpu.VMEM((4, 2, 256, 512), BF16),
            pltpu.VMEM((256, 256), BF16),
            pltpu.VMEM((256, 256), BF16),
            pltpu.VMEM((2, 256, 256), F32),
            pltpu.VMEM((2, 256, 256), F32),
            pltpu.VMEM((2, 256, 256), F32),
            pltpu.VMEM((4, 4, 8, 2, 16, 256), BF16),
            pltpu.VMEM((4, 4, 8, 16, 256), BF16),
            pltpu.VMEM((2, 4, 2, 256, 256), BF16),
            pltpu.VMEM((4, 256, 256), BF16),
            pltpu.VMEM((3, 512, 512), BF16),
            pltpu.VMEM((2, 2, 2, 2, 128, 256), BF16),
            pltpu.VMEM((4, 2, 2, 128, 256), BF16),
            pltpu.VMEM((3, 2, 2, 128, 256), BF16),
            pltpu.VMEM((2, 2, 2, 2, 128, 256), BF16),
            pltpu.VMEM((2, 2, 2, 2, 2, 128, 256), BF16),
            pltpu.VMEM((2, 2, 128, 256), BF16),
            pltpu.VMEM((2, 2, 2, 128, 256), BF16),
            pltpu.VMEM((3, 256, 512), F32),
            pltpu.VMEM((4, 512, 512), F32),
            dma((14,)),
            dma((352,)),
            dma((352,)),
        ],
        compiler_params=pltpu.CompilerParams(
            collective_id=0, has_side_effects=True, vmem_limit_bytes=limit
        ),
    )(
        stretch_nbrs.T,
        nbr_blocks,
        hidden,
        flat_enc,
        out_cotangent,
        key_weight,
        value_weight,
        query_weight,
        out_weight,
    )
    outs = pl.pallas_call(
        copy_kernel,
        out_shape=results,
        in_specs=[hbm()] * 7,
        out_specs=[hbm()] * 7,
        scratch_shapes=[pltpu.VMEM(r.shape, F32) for r in results] + [dma((2, 7))],
        compiler_params=pltpu.CompilerParams(vmem_limit_bytes=limit),
    )(*outs)
    layer_out, grad_hidden, grad_enc, grad_wq, grad_wk, grad_wv, grad_wo = outs
    return (
        layer_out,
        grad_hidden,
        grad_enc.reshape(encodings.shape),
        grad_wq,
        grad_wk,
        grad_wv,
        grad_wo,
    )


def solution(mesh):
    in_specs = (
        P("dp", "enc"),
        P("dp", None, "enc"),
        P("enc", None),
        P("enc", None),
        P("enc", None),
        P(None, "enc"),
        P("dp", "enc"),
        P("dp", None),
        P(),
    )
    out_specs = (
        P("dp", "enc"),
        P("dp", "enc"),
        P("dp", None, "enc"),
        P("enc", "dp"),
        P("enc", "dp"),
        P("enc", "dp"),
        P("dp", "enc"),
    )
    return jax.shard_map(
        per_device, mesh=mesh, in_specs=in_specs, out_specs=out_specs, check_vma=False
    )
```

```python
import functools

import jax
import jax.numpy as jnp
from jax import lax
from jax.experimental import pallas as pl
from jax.experimental.pallas import tpu as pltpu
from jax.sharding import PartitionSpec as P

HD = 128
BLK = 16
MESH = pl.DeviceIdType.MESH
F32 = jnp.float32
BF16 = jnp.bfloat16
NT = (((1,), (1,)), ((), ()))
TN = (((0,), (0,)), ((), ()))


def mm(a, b):
    return jnp.dot(a, b, preferred_element_type=F32)


class Place:
    def __init__(self):
        self.dp = lax.axis_index("dp")
        self.enc = lax.axis_index("enc")
        dp, enc = self.dp, self.enc
        self.y, self.c = dp // 2, dp % 2
        self.x, self.z = enc // 4, enc % 4
        x, y, z, c = self.x, self.y, self.z, self.c
        self.right = {
            "x": (dp, ((x + 1) % 4) * 4 + z),
            "z": (dp, x * 4 + (z + 1) % 4),
            "y": (((y + 1) % 4) * 2 + c, enc),
        }
        self.left = {
            "x": (dp, ((x + 3) % 4) * 4 + z),
            "z": (dp, x * 4 + (z + 3) % 4),
            "y": (((y + 3) % 4) * 2 + c, enc),
        }
        self.pos = {"x": x, "y": y, "z": z}
        self.partner = (y * 2 + (1 - c), enc)
        self.near = list(self.right.values()) + list(self.left.values()) + [self.partner]

    def column(self):
        steps = [(0, 1), (1, 0), (3, 0), (1, 1), (3, 1), (2, 0), (2, 1)]
        return [((self.y + dy) % 4, 1 - self.c if dc else self.c) for dy, dc in steps]

    def greet(self, others):
        sem = pltpu.get_barrier_semaphore()
        for other in others:
            pl.semaphore_signal(sem, inc=1, device_id=other, device_id_type=MESH)

    def meet(self, others):
        pl.semaphore_wait(pltpu.get_barrier_semaphore(), len(others))


class Copies:
    def __init__(self, send_sems, recv_sems):
        self.send_sems, self.recv_sems, self.used, self.started = send_sems, recv_sems, 0, []

    def start(self, src, dst, device):
        k = self.used
        self.used += 1
        copy = pltpu.make_async_remote_copy(
            src_ref=src,
            dst_ref=dst,
            send_sem=self.send_sems.at[k],
            recv_sem=self.recv_sems.at[k],
            device_id=device,
            device_id_type=MESH,
        )
        copy.start()
        self.started.append(copy)
        return copy

    def flush(self, some):
        for copy in some:
            copy.wait_send()
        gone = [id(copy) for copy in some]
        self.started = [copy for copy in self.started if id(copy) not in gone]

    def finish(self):
        self.flush(list(self.started))


class RingSum:
    def __init__(self, copies, place, axis, part, r1, r2):
        self.copies, self.part, self.r1, self.r2 = copies, part, r1, r2
        self.right, self.left = place.right[axis], place.left[axis]
        pos = place.pos[axis]
        self.pos, self.rt, self.lf, self.opp = pos, (pos + 1) % 4, (pos + 3) % 4, (pos + 2) % 4

    def send_opposite(self):
        self.a = self.copies.start(self.part(self.opp, 0), self.r1.at[0], self.right)
        self.b = self.copies.start(self.part(self.opp, 1), self.r1.at[1], self.left)

    def send_right(self):
        self.d = self.copies.start(self.part(self.rt, 1), self.r2.at[0, 1], self.right)

    def send_left(self):
        self.e = self.copies.start(self.part(self.lf, 0), self.r2.at[1, 0], self.left)

    def first(self):
        self.send_opposite()
        self.send_right()
        self.send_left()

    def second(self):
        self.a.wait_recv()
        mine = self.part(self.rt, 0)
        mine[...] = (mine[...].astype(F32) + self.r1[0].astype(F32)).astype(BF16)
        self.f = self.copies.start(mine, self.r2.at[0, 0], self.right)
        self.b.wait_recv()
        mine = self.part(self.lf, 1)
        mine[...] = (mine[...].astype(F32) + self.r1[1].astype(F32)).astype(BF16)
        self.g = self.copies.start(mine, self.r2.at[1, 1], self.left)

    def flush(self):
        self.copies.flush([self.a, self.b, self.d, self.e, self.f, self.g])

    def total(self):
        for copy in (self.d, self.e, self.f, self.g):
            copy.wait_recv()
        return [
            self.part(self.pos, h)[...].astype(F32)
            + self.r2[0, h].astype(F32)
            + self.r2[1, h].astype(F32)
            for h in (0, 1)
        ]


class RingGather:
    def __init__(self, copies, place, axis, block):
        self.copies, self.block = copies, block
        self.right, self.left = place.right[axis], place.left[axis]
        pos = place.pos[axis]
        self.pos, self.rt, self.lf = pos, (pos + 1) % 4, (pos + 3) % 4

    def first(self):
        own = self.block(self.pos, None)
        self.a = self.copies.start(own, own, self.right)
        self.b = self.copies.start(own, own, self.left)

    def second(self):
        self.a.wait_recv()
        part = self.block(self.lf, 0)
        self.d = self.copies.start(part, part, self.right)
        self.b.wait_recv()
        part = self.block(self.rt, 1)
        self.e = self.copies.start(part, part, self.left)

    def done(self):
        self.d.wait_recv()
        self.e.wait_recv()

    def flush(self):
        self.copies.flush([self.a, self.b, self.d, self.e])


HALVES = ((0, 128), (128, 256))


class PlaneSum:
    def __init__(self, copies, place, terms, sums, r1a, r2a, r1b, r2b):
        x, z = place.pos["x"], place.pos["z"]
        self.sums, self.place = sums, place

        def upper(b, h):
            return terms.at[b, 2 * h : 2 * h + 2, 0:128]

        def lower(b, h):
            return terms.at[2 * h : 2 * h + 2, b, 128:256]

        self.one = (
            RingSum(copies, place, "x", upper, r1a.at[0], r2a.at[0]),
            RingSum(copies, place, "z", lower, r1a.at[1], r2a.at[1]),
        )

        def upper_two(b, h):
            return sums.at[0, b, 64 * h : 64 * h + 64]

        def lower_two(b, h):
            return sums.at[1, b, 64 * h : 64 * h + 64]

        self.two = (
            RingSum(copies, place, "z", upper_two, r1b.at[0], r2b.at[0]),
            RingSum(copies, place, "x", lower_two, r1b.at[1], r2b.at[1]),
        )

    def opposite(self):
        for ring in self.one:
            ring.send_opposite()

    def sides(self):
        for ring in self.one:
            ring.send_right()
            ring.send_left()

    def step2(self):
        for ring in self.one:
            ring.second()

    def step3(self):
        for k in (0, 1):
            low, high = self.one[k].total()
            self.sums[k, 0:2] = low.astype(BF16)
            self.sums[k, 2:4] = high.astype(BF16)
            self.two[k].first()

    def step4(self):
        for ring in self.one:
            ring.flush()
        for ring in self.two:
            ring.second()

    def finish(self, store):
        for k in (0, 1):
            low, high = self.two[k].total()
            store(k * 128, low.astype(BF16))
            store(k * 128 + 64, high.astype(BF16))


class PlaneGather:
    def __init__(self, copies, place, buf):
        self.copies = copies
        half = buf.shape[2] // 2
        self.ways = [self.way(copies, place, buf, half, k) for k in (0, 1)]

    def way(self, copies, place, buf, half, k):
        axes = ("x", "z") if k == 0 else ("z", "x")
        near, far = [place.pos[axis] for axis in axes]
        quarter = half // 2
        start = k * half

        def cells(i, j, rows):
            return buf.at[i, j, rows] if k == 0 else buf.at[j, i, rows]

        def block(b, h):
            if h is None:
                return cells(b, far, slice(start, start + half))
            low = start + quarter * h
            return cells(b, far, slice(low, low + quarter))

        def pair_of(h, j):
            return cells(slice(2 * h, 2 * h + 2), j, slice(start, start + half))

        return {
            "ring": RingGather(copies, place, axes[0], block),
            "block": block,
            "pair": pair_of,
            "near": near,
            "far": far,
            "right": place.right[axes[1]],
            "left": place.left[axes[1]],
            "from_left": [],
            "from_right": [],
        }

    def send(self, way, step):
        cell = way["block"]((way["near"] + step) % 4, None)
        way["from_left"].append(self.copies.start(cell, cell, way["right"]))
        way["from_right"].append(self.copies.start(cell, cell, way["left"]))

    def step1(self):
        for way in self.ways:
            way["ring"].first()
        for way in self.ways:
            self.send(way, 0)

    def step2(self):
        for way in self.ways:
            way["ring"].second()
        for way in self.ways:
            self.send(way, 1)
            self.send(way, 3)

    def step3(self):
        for way in self.ways:
            way["ring"].done()
            self.send(way, 2)

    def step4(self):
        for way in self.ways:
            for copy in way["from_left"]:
                copy.wait_recv()
            part = way["pair"](0, (way["far"] + 3) % 4)
            way["d"] = self.copies.start(part, part, way["right"])
            for copy in way["from_right"]:
                copy.wait_recv()
            part = way["pair"](1, (way["far"] + 1) % 4)
            way["e"] = self.copies.start(part, part, way["left"])

    def done(self):
        for way in self.ways:
            way["d"].wait_recv()
            way["e"].wait_recv()


def layer_kernel(
    nbrs,
    blocks,
    hidden,
    encodings,
    cotangent,
    wk_hbm,
    wv_hbm,
    wq_hbm,
    wo_hbm,
    layer_hbm,
    grad_hidden_hbm,
    grad_encodings_hbm,
    grad_wq_hbm,
    grad_wk_hbm,
    grad_wv_hbm,
    grad_wo_hbm,
    weights,
    out_weight,
    terms,
    sums,
    r1a,
    r2a,
    r1b,
    r2b,
    pair,
    cots,
    encs,
    hids,
    queries,
    grads,
    prob,
    scored,
    flipped,
    spread_v,
    spread_q,
    theirs,
    theirs_q,
    side_t,
    dense_in,
    dense_sum,
    dense_r,
    part_r1,
    part_r2,
    half_r1,
    half_r2,
    rows_out,
    grads_out,
    load_sems,
    send_sems,
    recv_sems,
):
    place = Place()
    x, y, z, c = place.x, place.y, place.z, place.c
    copies = Copies(send_sems, recv_sems)
    column = place.column()
    met = place.near + [(oy * 2 + oc, place.enc) for oy, oc in column[3:]]
    loads = [
        pltpu.make_async_copy(src, dst, load_sems.at[k])
        for k, (src, dst) in enumerate(
            [
                (wv_hbm, weights.at[1]),
                (wq_hbm, weights.at[2]),
                (wo_hbm, out_weight),
            ]
        )
    ]
    pieces = [
        pltpu.make_async_copy(
            wk_hbm.at[:, 1024 * b : 1024 * b + 1024],
            weights.at[0, :, 1024 * b : 1024 * b + 1024],
            load_sems.at[10 + b],
        )
        for b in range(4)
    ]
    for piece in pieces:
        piece.start()
    loads[0].start()
    place.greet(met)
    results = [
        pltpu.make_async_copy(src, dst, load_sems.at[3 + k])
        for k, (src, dst) in enumerate(
            [
                (rows_out.at[0], layer_hbm),
                (rows_out.at[1], grad_hidden_hbm),
                (rows_out.at[2], grad_encodings_hbm),
                (grads_out.at[0], grad_wq_hbm),
                (grads_out.at[1], grad_wk_hbm),
                (grads_out.at[2], grad_wv_hbm),
                (grads_out.at[3], grad_wo_hbm),
            ]
        )
    ]

    left = (encodings, encodings, hidden)
    keys, values, query, grad = [
        PlaneSum(
            copies, place, terms.at[k], sums.at[k], r1a.at[k], r2a.at[k], r1b.at[k], r2b.at[k]
        )
        for k in range(4)
    ]

    def first_terms():
        for b in range(4):
            pieces[b].wait()
            product = mm(encodings[...], weights[0, :, 1024 * b : 1024 * b + 1024]).astype(BF16)
            for i in range(4):
                terms[0, b, i] = product[:, i * 256 : i * 256 + 256]
        loads[1].start()
        loads[2].start()

    def make_terms(k):
        loads[k - 1].wait()
        rows = left[k][...]

        def body(b, carry):
            product = mm(rows, weights[k, :, columns(b)]).astype(BF16)
            for i in range(4):
                terms[k, b, i] = product[:, i * 256 : i * 256 + 256]
            return carry

        lax.fori_loop(0, 4, body, 0)

    def make_grad_terms():
        loads[2].wait()
        rows = cotangent[...]

        def body(b, carry):
            for i in range(4):
                span = pl.ds(pl.multiple_of(b * 1024 + i * 256, 256), 256)
                product = lax.dot_general(rows, out_weight[span, :], NT, preferred_element_type=F32)
                terms[3, b, i] = product.astype(BF16)
            return carry

        lax.fori_loop(0, 4, body, 0)

    def columns(b):
        return pl.ds(pl.multiple_of(b * 1024, 1024), 1024)

    def row_block(ref):
        def block(b, h):
            if h is None:
                return ref.at[b, c]
            return ref.at[b, c, 128 * h : 128 * h + 128]

        return block

    def pair_block(k):
        def block(b, h):
            if h is None:
                return pair.at[k, b, c]
            return pair.at[k, b, c, h]

        return block

    gather_encs = RingGather(copies, place, "y", row_block(encs))
    gather_hids = RingGather(copies, place, "y", row_block(hids))
    gather_keys, gather_values = [
        RingGather(copies, place, "y", pair_block(k)) for k in (0, 1)
    ]

    def swap(gather, mine):
        gather.done()
        return copies.start(mine, mine, place.partner)

    def store_pair(k):
        def store(row, value):
            at = row % 128
            pair[k, y, c, row // 128, at : at + 64] = value

        return store

    def store_to(ref):
        def store(row, value):
            ref[row : row + 64] = value

        return store

    scale = HD ** (-0.5)
    cases = [(t, h) for t in range(4) for h in range(2)]

    def rows_of(ref, t, h):
        return ref[t * 64 : t * 64 + 64, h * 128 : h * 128 + 128]

    def picked(which, t, h):
        return jnp.concatenate(
            [
                pair[which, n // 4, (n // 2) % 2, n % 2, :, h * 128 : h * 128 + 128]
                for n in (nbrs[0, t], nbrs[1, t])
            ],
            axis=0,
        )

    def attend():
        slot = lax.broadcasted_iota(jnp.int32, (64, 256), 1)
        for i, (t, h) in enumerate(cases):
            limit0 = BLK * blocks[nbrs[0, t]]
            limit1 = BLK * blocks[nbrs[1, t]]
            valid = slot < jnp.where(slot < 128, limit0, limit1 + 128)
            scores = (
                lax.dot_general(
                    rows_of(queries, t, h), picked(0, t, h), NT, preferred_element_type=F32
                )
                * scale
            )
            scores = jnp.where(valid, scores, -1e30)
            top = jnp.max(scores, axis=1, keepdims=True)
            exps = jnp.where(valid, jnp.exp(scores - top), 0.0)
            total = jnp.sum(exps, axis=1, keepdims=True)
            output = mm(exps.astype(BF16), picked(1, t, h)) / total
            terms[0, x, z, t * 64 : t * 64 + 64, h * 128 : h * 128 + 128] = output.astype(BF16)
            prob[h, t * 64 : t * 64 + 64] = exps / total

    def attend_back():
        for t, h in cases:
            weight = prob[h, t * 64 : t * 64 + 64]
            grad_prob = lax.dot_general(
                rows_of(grads, t, h), picked(1, t, h), NT, preferred_element_type=F32
            )
            inner = jnp.sum(weight * grad_prob, axis=1, keepdims=True)
            found = weight * (grad_prob - inner) * scale
            scored[h, t * 64 : t * 64 + 64] = found
            term = mm(found.astype(BF16), picked(0, t, h))
            terms[1, x, z, t * 64 : t * 64 + 64, h * 128 : h * 128 + 128] = term.astype(BF16)

    def flip(source):
        for h in range(2):
            flipped[h] = source[h].T

    def neighbour_grads(which, rows):
        lane = lax.broadcasted_iota(jnp.int32, (128, 256), 1)
        names = []
        for j in range(2):
            name = jnp.where(lane < 64, nbrs[j, 0], nbrs[j, 1])
            name = jnp.where(lane < 128, name, nbrs[j, 2])
            names.append(jnp.where(lane < 192, name, nbrs[j, 3]))

        def body(i, carry):
            for h in range(2):
                first, second = flipped[h, 0:128], flipped[h, 128:256]
                chosen = jnp.concatenate(
                    [
                        jnp.where(
                            names[0] == n,
                            first,
                            jnp.where(names[1] == n, second, jnp.zeros_like(first)),
                        )
                        for n in (2 * i, 2 * i + 1)
                    ],
                    axis=0,
                ).astype(BF16)
                term = mm(chosen, rows[:, h * 128 : h * 128 + 128]).astype(BF16)
                for j in range(2):
                    sums[
                        2 * which + i // 4, (i // 2) % 2, 2 * (i % 2) + j, :, h * 128 : h * 128 + 128
                    ] = term[j * 128 : j * 128 + 128]
            return carry

        lax.fori_loop(0, 8, body, 0)

    def swap_dense(k):
        return copies.start(
            sums.at[2 * k : 2 * k + 2, :, pl.ds(2 * (1 - c), 2)], dense_in.at[k], place.partner
        )

    def send_dense(k, swapped):
        swapped.wait_recv()
        for b in range(4):
            mine = sums[2 * k + b // 2, b % 2, pl.ds(2 * c, 2)]
            theirs_too = dense_in[k, b // 2, b % 2]
            dense_sum[b, k] = (mine.astype(F32) + theirs_too.astype(F32)).astype(BF16)
        return [
            copies.start(
                dense_sum.at[(y + step) % 4, k],
                dense_r.at[i, k],
                (((y + step) % 4) * 2 + c, place.enc),
            )
            for i, step in enumerate((1, 3, 2))
        ]

    def sum_dense(k, moves):
        for move in moves:
            move.wait_recv()
        total = dense_sum[y, k].astype(F32)
        for i in range(3):
            total = total + dense_r[i, k].astype(F32)
        terms[2 + k, x, z] = total.astype(BF16).reshape(256, 256)

    net_h, net_q, net_k, net_v = [PlaneGather(copies, place, terms.at[k]) for k in range(4)]
    net_sv, net_sq = [PlaneGather(copies, place, ref) for ref in (spread_v, spread_q)]

    def swap_half(k):
        return copies.start(terms.at[2 * k, :, pl.ds(2 * (1 - c), 2)], theirs.at[k], place.partner)

    class WeightGrad:
        def __init__(self, k):
            def part(b, h):
                return r2a.at[2 * k + b // 2, b % 2, h]

            self.k = k
            self.ring = RingSum(copies, place, "y", part, part_r1.at[k], part_r2.at[k])

        def block(self, b):
            k = self.k
            own = jnp.concatenate([terms[2 * k, b, 2 * c + i] for i in (0, 1)], axis=1)
            other = jnp.concatenate([theirs[k, b, i] for i in (0, 1)], axis=1)
            both = jnp.concatenate([own, other], axis=0)
            product = mm(side_t[2 * k], both).astype(BF16)
            for h in (0, 1):
                for i in (0, 1):
                    quarter = product[256 * h : 256 * h + 256, 256 * i : 256 * i + 256]
                    r2a[2 * k + b // 2, b % 2, h, i] = quarter.reshape(2, 128, 256)

        def one(self):
            self.block(self.ring.opp)
            self.ring.send_opposite()

        def two(self):
            self.block(self.ring.rt)
            self.ring.send_right()

        def three(self):
            self.block(self.ring.lf)
            self.ring.send_left()

        def four(self):
            self.block(self.ring.pos)

        def store(self):
            for h, found in enumerate(self.ring.total()):
                for i in (0, 1):
                    square = found[i].reshape(256, 256)
                    if self.k == 0:
                        grads_out[3, 256 * i : 256 * i + 256, 256 * h : 256 * h + 256] = square.T
                    else:
                        grads_out[1, 256 * h : 256 * h + 256, 256 * i : 256 * i + 256] = square
            results[6 if self.k == 0 else 4].start()

    class QueryGrad(WeightGrad):
        def __init__(self):
            def part(b, h):
                return pair.at[0, b, h]

            self.ring = RingSum(copies, place, "y", part, half_r1, half_r2)

        def block(self, b):
            both = jnp.concatenate([terms[1, b, 2 * c], theirs_q[b]], axis=0)
            product = mm(side_t[1], both).astype(BF16)
            pair[0, b] = product.reshape(2, 2, 128, 256)

        def store(self):
            for h, found in enumerate(self.ring.total()):
                grads_out[0, 256 * h : 256 * h + 256, 0:256] = found.reshape(256, 256)

    def wide(k, b):
        return jnp.concatenate([terms[k, b, i] for i in range(4)], axis=1)

    def accumulate(k, make, add=False, last=True):
        def body(b, carry):
            rows_out[k] += make(b)
            return carry

        if not add:
            rows_out[k] = make(0)
        lax.fori_loop(0 if add else 1, 4, body, 0)
        if last:
            results[k].start()

    def transposed(k, slot, b):
        return lax.dot_general(
            wide(k, b), weights[slot, :, columns(b)], NT, preferred_element_type=F32
        )

    def turn(source, store):
        def body(t, carry):
            rows = []
            for e in (2 * t, 2 * t + 1):
                span = pl.ds(pl.multiple_of(e * 16, 16), 16)
                rows += [source[d // 2, d % 2, span] for d in range(8)]
            store(t, jnp.concatenate(rows, axis=0).T)
            return carry

        lax.fori_loop(0, 8, body, 0)

    def store_encs(t, found):
        for i in range(4):
            r1a[t // 2, t % 2, i // 2, i % 2] = found[128 * i : 128 * i + 128]

    def store_hids(t, found):
        for i in range(4):
            sums[t // 2, t % 2, i] = found[128 * i : 128 * i + 128]

    def exchange_values():
        span = pl.ds(pl.multiple_of(place.enc * 16, 16), 16)
        spread_v[x, z, place.dp] = terms[3, y, pl.ds(2 * c, 2), span]
        return [
            copies.start(
                terms.at[3, oy, pl.ds(2 * oc, 2), span],
                spread_v.at[x, z, place.dp],
                (oy * 2 + oc, place.enc),
            )
            for oy, oc in column
        ]

    def exchange_queries():
        span = pl.ds(pl.multiple_of(place.enc * 16, 16), 16)
        spread_q[x, z, place.dp] = terms[1, y, 2 * c + 1, span]
        return [
            copies.start(
                terms.at[1, oy, 2 * oc + 1, span],
                spread_q.at[x, z, place.dp],
                (oy * 2 + oc, place.enc),
            )
            for oy, oc in column
        ]

    def whole_grad(turned, rows_of_part):
        total = None
        for b in range(4):
            sides = jnp.concatenate(
                [
                    jnp.concatenate([turned(b, j, i) for j in (0, 1)], axis=1)
                    for i in range(4)
                ],
                axis=0,
            )
            rows = jnp.concatenate([rows_of_part(b, k) for k in range(4)], axis=0)
            term = mm(sides, rows)
            total = term if total is None else total + term
        return total

    def value_rows(b, k):
        return jnp.concatenate([spread_v[b, k, :, i].reshape(128, 256) for i in (0, 1)], axis=1)

    def query_rows(b, k):
        return spread_q[b, k].reshape(128, 256)

    def turned_encs(b, j, i):
        return r1a[b, j, i // 2, i % 2]

    def turned_hids(b, j, i):
        return sums[b, j, i]

    cots[0] = cotangent[...]
    encs[y, c] = encodings[...]
    hids[y, c] = hidden[...]
    work_h, work_k, work_q = WeightGrad(0), WeightGrad(1), QueryGrad()
    first_terms()
    place.meet(met)
    keys.opposite()
    gather_hids.first()
    keys.sides()
    make_terms(1)
    keys.step2()
    values.opposite()
    make_grad_terms()
    gather_encs.first()
    values.sides()
    gather_hids.second()
    keys.step3()
    make_terms(2)
    values.step2()
    keys.step4()
    query.opposite()
    values.step3()
    keys.finish(store_pair(0))
    query.sides()
    gather_encs.second()
    gather_keys.first()
    values.step4()
    swap_hids = swap(gather_hids, hids.at[:, c])
    query.step2()
    grad.opposite()
    values.finish(store_pair(1))
    gather_keys.second()
    swap_cots = copies.start(cots.at[0], cots.at[1], place.partner)
    gather_values.first()
    grad.sides()
    query.step3()
    swap_cots.wait_recv()
    for k in (0, 1):
        side_t[0, :, k * 256 : k * 256 + 256] = cots[k].T
    grad.step2()
    swap_keys = swap(gather_keys, pair.at[0, :, c])
    gather_values.second()
    query.step4()
    swap_encs = swap(gather_encs, encs.at[:, c])
    swap_values = swap(gather_values, pair.at[1, :, c])
    grad.step3()
    query.finish(store_to(queries))
    swap_keys.wait_recv()
    swap_values.wait_recv()
    attend()
    grad.step4()
    net_h.step1()
    swap_hids.wait_recv()
    side_t[1, :, 0:256] = hids[y, c].T
    side_t[1, :, 256:512] = hids[y, 1 - c].T
    flip(prob)
    grad.finish(store_to(grads))
    net_h.step2()
    attend_back()
    for total in (keys, values, query, grad):
        for ring in total.two:
            ring.flush()
    net_h.step3()
    neighbour_grads(1, grads)
    swap_dense_v = swap_dense(1)
    net_q.step1()
    flip(scored)
    neighbour_grads(0, queries)
    swap_dense_k = swap_dense(0)
    net_h.step4()
    moves_dv = send_dense(1, swap_dense_v)
    net_q.step2()
    moves_dk = send_dense(0, swap_dense_k)
    swap_encs.wait_recv()
    side_t[2, :, 0:256] = encs[y, c].T
    side_t[2, :, 256:512] = encs[y, 1 - c].T
    net_h.done()
    swap_h = swap_half(0)
    net_q.step3()
    sum_dense(1, moves_dv)
    net_v.step1()
    swap_h.wait_recv()
    work_h.one()
    net_q.step4()
    gather_keys.flush()
    gather_values.flush()
    copies.flush([swap_keys, swap_values])
    sum_dense(0, moves_dk)
    work_h.two()
    net_k.step1()
    net_v.step2()
    work_h.three()
    net_q.done()
    moves_q = exchange_queries()
    swap_q = copies.start(terms.at[1, :, 2 * (1 - c)], theirs_q, place.partner)
    net_k.step2()
    work_h.ring.second()
    accumulate(0, lambda b: mm(wide(0, b), out_weight[columns(b), :]))
    swap_q.wait_recv()
    work_q.one()
    work_q.two()
    net_k.step3()
    net_v.step3()
    copies.flush([swap_dense_v, swap_dense_k])
    turn(hids, store_hids)
    work_h.four()
    turn(encs, store_encs)
    work_q.three()
    net_k.step4()
    net_v.step4()
    for move in moves_q:
        move.wait_recv()
    net_sq.step1()
    accumulate(1, lambda b: transposed(1, 2, b))
    work_q.ring.second()
    net_k.done()
    work_q.four()
    swap_k = swap_half(1)
    net_v.done()
    moves_v = exchange_values()
    net_sq.step2()
    swap_k.wait_recv()
    work_k.one()
    for move in moves_v:
        move.wait_recv()
    net_sv.step1()
    work_k.two()
    net_sq.step3()
    work_k.three()
    work_h.store()
    net_sv.step2()
    net_sv.step3()
    work_k.ring.second()
    work_q.store()
    net_sq.step4()
    accumulate(2, lambda b: transposed(3, 1, b), last=False)
    net_sv.step4()
    net_sq.done()
    work_k.four()
    grads_out[0, :, 256:512] = whole_grad(turned_hids, query_rows)
    accumulate(2, lambda b: transposed(2, 0, b), add=True)
    net_sv.done()
    results[3].start()
    grads_out[2] = whole_grad(turned_encs, value_rows)
    results[5].start()
    work_k.store()
    for k in range(7):
        results[k].wait()
    copies.finish()


def copy_kernel(*refs):
    sems = refs[-1]
    count = (len(refs) - 1) // 3
    loads, moves = [], []
    for k in range(count):
        held = refs[2 * count + k]
        loads.append(pltpu.make_async_copy(refs[k], held, sems.at[0, k]))
        moves.append(pltpu.make_async_copy(held, refs[count + k], sems.at[1, k]))
    for load in loads:
        load.start()
    for load, move in zip(loads, moves):
        load.wait()
        move.start()
    for move in moves:
        move.wait()


def vmem():
    return pl.BlockSpec(memory_space=pltpu.VMEM)


def hbm():
    return pl.BlockSpec(memory_space=pl.ANY)


def shape(*dims, dtype=BF16):
    return jax.ShapeDtypeStruct(dims, dtype)


def per_device(
    hidden,
    encodings,
    query_weight,
    key_weight,
    value_weight,
    out_weight,
    out_cotangent,
    stretch_nbrs,
    nbr_blocks,
):
    flat_enc = encodings.reshape(256, 512)
    dma = pltpu.SemaphoreType.DMA
    limit = 62 * 1024 * 1024
    results = [shape(256, 512, dtype=F32)] * 3 + [shape(512, 512, dtype=F32)] * 4
    outs = pl.pallas_call(
        layer_kernel,
        out_shape=results,
        in_specs=[pl.BlockSpec(memory_space=pltpu.SMEM)] * 2 + [vmem()] * 3 + [hbm()] * 4,
        out_specs=[hbm()] * 7,
        scratch_shapes=[
            pltpu.VMEM((3, 512, 4096), BF16),
            pltpu.VMEM((4096, 512), BF16),
            pltpu.VMEM((4, 4, 4, 256, 256), BF16),
            pltpu.VMEM((4, 2, 4, 128, 256), BF16),
            pltpu.VMEM((4, 2, 2, 2, 128, 256), BF16),
            pltpu.VMEM((4, 2, 2, 2, 2, 128, 256), BF16),
            pltpu.VMEM((4, 2, 2, 64, 256), BF16),
            pltpu.VMEM((4, 2, 2, 2, 64, 256), BF16),
            pltpu.VMEM((2, 4, 2, 2, 128, 256), BF16),
            pltpu.VMEM((2, 256, 512), BF16),
            pltpu.VMEM((4, 2, 256, 512), BF16),
            pltpu.VMEM((4, 2, 256, 512), BF16),
            pltpu.VMEM((256, 256), BF16),
            pltpu.VMEM((256, 256), BF16),
            pltpu.VMEM((2, 256, 256), F32),
            pltpu.VMEM((2, 256, 256), F32),
            pltpu.VMEM((2, 256, 256), F32),
            pltpu.VMEM((4, 4, 8, 2, 16, 256), BF16),
            pltpu.VMEM((4, 4, 8, 16, 256), BF16),
            pltpu.VMEM((2, 4, 2, 256, 256), BF16),
            pltpu.VMEM((4, 256, 256), BF16),
            pltpu.VMEM((3, 512, 512), BF16),
            pltpu.VMEM((2, 2, 2, 2, 128, 256), BF16),
            pltpu.VMEM((4, 2, 2, 128, 256), BF16),
            pltpu.VMEM((3, 2, 2, 128, 256), BF16),
            pltpu.VMEM((2, 2, 2, 2, 128, 256), BF16),
            pltpu.VMEM((2, 2, 2, 2, 2, 128, 256), BF16),
            pltpu.VMEM((2, 2, 128, 256), BF16),
            pltpu.VMEM((2, 2, 2, 128, 256), BF16),
            pltpu.VMEM((3, 256, 512), F32),
            pltpu.VMEM((4, 512, 512), F32),
            dma((14,)),
            dma((352,)),
            dma((352,)),
        ],
        compiler_params=pltpu.CompilerParams(
            collective_id=0, has_side_effects=True, vmem_limit_bytes=limit
        ),
    )(
        stretch_nbrs.T,
        nbr_blocks,
        hidden,
        flat_enc,
        out_cotangent,
        key_weight,
        value_weight,
        query_weight,
        out_weight,
    )
    outs = pl.pallas_call(
        copy_kernel,
        out_shape=results,
        in_specs=[hbm()] * 7,
        out_specs=[hbm()] * 7,
        scratch_shapes=[pltpu.VMEM(r.shape, F32) for r in results] + [dma((2, 7))],
        compiler_params=pltpu.CompilerParams(vmem_limit_bytes=limit),
    )(*outs)
    layer_out, grad_hidden, grad_enc, grad_wq, grad_wk, grad_wv, grad_wo = outs
    return (
        layer_out,
        grad_hidden,
        grad_enc.reshape(encodings.shape),
        grad_wq,
        grad_wk,
        grad_wv,
        grad_wo,
    )


def solution(mesh):
    in_specs = (
        P("dp", "enc"),
        P("dp", None, "enc"),
        P("enc", None),
        P("enc", None),
        P("enc", None),
        P(None, "enc"),
        P("dp", "enc"),
        P("dp", None),
        P(),
    )
    out_specs = (
        P("dp", "enc"),
        P("dp", "enc"),
        P("dp", None, "enc"),
        P("enc", "dp"),
        P("enc", "dp"),
        P("enc", "dp"),
        P("dp", "enc"),
    )
    return jax.shard_map(
        per_device, mesh=mesh, in_specs=in_specs, out_specs=out_specs, check_vma=False
    )
```
